32 devices in a mesh: px: 8 (over y, x, core), py: 4 (over z).
Axes of the slice: x: 2, y: 2, z: 4, core: 2. Of those that a mesh axis runs over, the one named last changes fastest.
Arguments:
- displacement: float32 [60, 16, 8, 128], P(None, 'px', 'py'), may hold values from -4 to 4
- velocity: float32 [60, 16, 8, 128], P(None, 'px', 'py'), may hold values from -6 to 6
- modulus: float32 [16, 8, 128], P('px', 'py'), may hold values from 0.5 to 4
- gradient_map: float32 [243, 60], replicated, may hold values from -0.75 to 0.75
- trace_map: float32 [6, 54, 60], replicated, may hold values from -0.75 to 0.75
- lift_map: float32 [6, 60, 54], replicated, may hold values from -0.3125 to 0.3125
- split_map: float32 [27, 27], replicated, may hold values from -1.25 to 1.25
- spread_map: float32 [6, 60, 27], replicated, may hold values from -1.25 to 1.25
- fracture_faces: int32 [32, 512], P(('px', 'py')), may hold values from 0 to 1534, as said below
- fracture_counts: int32 [32, 3], P(('px', 'py')), may hold values from 0 to 256, as said below
Outputs:
- displacement_out: float32 [60, 16, 8, 128], P(None, 'px', 'py')
- velocity_out: float32 [60, 16, 8, 128], P(None, 'px', 'py')
The draws below stay inside these ranges and needn't reach their ends.
Inputs may be any that keep to these rules, and one draw needn't show every extreme that they name: `fracture_faces`: row p holds the device at index p of px+py (px major). With local element numbers (i * 2 + j) * 128 + k and face ids d * 2 * 2 * 128 + element, slots 0 to 127 name +x faces of elements with i = 1, the next 128 slots +y faces of elements with j = 1, the last 256 slots faces whose neighbour lies on the same device. All ids of a row differ. Only the first fracture_counts[p, s] slots of section s open. `fracture_counts`: counts of opened slots in the three sections of a row. The first is 0 on devices with the last px index, the second on devices with the last py index; over all devices the sections reach 128, 128 and 256.
All inputs are finite; a program needn't handle non-finite values.
Results may differ from the reference program's by a relative error of at most 0.0003.
Values sent between devices are 32-bit elements; how exact they have to be, the bound alone decides.
A program may use at most 64 MiB of HBM per device.

```python
import math
import jax
import jax.numpy as jnp
from jax import lax

QUAD = 27
FACE_QUAD = 9
DOF = 60
CX = 2
CY = 2
EZ = 128
BLK_CAP = 128
LOC_CAP = 256
NX = 16
NY = 8
N_PX = 8
N_PY = 4
DEVICES = 32


def fracture_plan(key):
    base_key = jax.random.fold_in(key, 7)
    keys = jax.random.split(base_key, 9)
    device = jnp.arange(DEVICES, dtype=jnp.int32)
    device_x = device // N_PY
    device_y = device % N_PY
    x_raw = jax.random.randint(keys[0], (DEVICES,), 0, BLK_CAP + 1)
    x_full = jax.random.randint(keys[1], (), 0, (N_PX - 1) * N_PY)
    x_count = jnp.where(device == x_full, BLK_CAP, x_raw)
    x_count = jnp.where(device_x < N_PX - 1, x_count, 0)
    y_raw = jax.random.randint(keys[2], (DEVICES,), 0, BLK_CAP + 1)
    y_full = jax.random.randint(keys[3], (), 0, N_PX) * N_PY + jax.random.randint(keys[4], (), 0, N_PY - 1)
    y_count = jnp.where(device == y_full, BLK_CAP, y_raw)
    y_count = jnp.where(device_y < N_PY - 1, y_count, 0)
    first_draw = jax.random.randint(keys[5], (DEVICES,), 0, LOC_CAP + 1)
    second_draw = jax.random.randint(keys[6], (DEVICES,), 0, LOC_CAP + 1)
    local_count = first_draw * second_draw // LOC_CAP
    local_full = jax.random.randint(keys[7], (), 0, DEVICES)
    local_count = jnp.where(device == local_full, LOC_CAP, local_count)
    counts = jnp.stack([x_count, y_count, local_count], axis=1).astype(jnp.int32)
    elements = CX * CY * EZ
    device_keys = jax.random.split(keys[8], DEVICES)

    def one_device(device_key):
        key_x, key_y, key_local = jax.random.split(device_key, 3)
        spot_x = jax.random.permutation(key_x, CY * EZ)[:BLK_CAP]
        x_ids = (CX - 1) * CY * EZ + spot_x
        spot_y = jax.random.permutation(key_y, CX * EZ)[:BLK_CAP]
        y_ids = elements + (spot_y // EZ * CY + CY - 1) * EZ + spot_y % EZ
        candidate = jnp.arange(3 * elements, dtype=jnp.int32)
        direction = candidate // elements
        element = candidate % elements
        inner_face = (direction == 0) & (element // (CY * EZ) < CX - 1) | (direction == 1) & (element // EZ % CY < CY - 1) | (direction == 2) & (element % EZ < EZ - 1)
        rank_order = jax.random.permutation(key_local, 3 * elements).astype(jnp.int32)
        scores = jnp.where(inner_face, rank_order, rank_order + 3 * elements)
        fixed_face = (candidate == 0) | (candidate == 3 * elements - 2)
        scores = jnp.where(fixed_face, rank_order + 6 * elements, scores)
        chosen = jnp.argsort(scores, stable=True)[:LOC_CAP - 2]
        ends = jnp.array([0, 3 * elements - 2], dtype=jnp.int32)
        return jnp.concatenate([x_ids.astype(jnp.int32), y_ids.astype(jnp.int32), chosen.astype(jnp.int32), ends])
    faces = jax.vmap(one_device)(device_keys)
    return (faces.astype(jnp.int32), counts)


def draw_fracture_faces(key, part):
    return fracture_plan(key)[0]


def draw_fracture_counts(key, part):
    return fracture_plan(key)[1]


def block_scale(own_key, extent, pieces, least, largest):
    def one(position, blocks):
        steps = jax.random.uniform(jax.random.fold_in(jax.random.fold_in(own_key, 6), position), (blocks,), jnp.float32, least / len(pieces), largest / len(pieces))
        return jnp.repeat(jnp.exp(steps), extent[position] // blocks).reshape((-1,) + (1,) * (len(extent) - position - 1))

    gain = one(*pieces[0])
    for cut in pieces[1:]:
        gain = gain * one(*cut)
    return gain


def centred(stream_key, dims, width, limit, cuts=(), held_as=jnp.bfloat16):
    values = jax.random.normal(stream_key, dims, jnp.float32) * width
    if len(cuts) > 0:
        values = block_scale(stream_key, dims, cuts, -0.22, 0.18) * values
    return jnp.clip(values, min=-limit, max=limit).astype(held_as)


def setup_inputs(seed: int = 0) -> dict:
    arg_keys = jax.random.split(jax.random.key(seed), 11)
    displacement = centred(arg_keys[0], (DOF, NX, NY, EZ), 0.5, 4.0, ((1, 8), (2, 4)), jnp.float32)
    velocity = centred(arg_keys[1], (DOF, NX, NY, EZ), 1.0, 6.0, ((1, 8), (2, 4)), jnp.float32)
    modulus = jnp.clip(jnp.exp(math.log(4.0) - 2.0794415 * jax.random.uniform(arg_keys[2], (NX, NY, EZ), jnp.float32) ** block_scale(arg_keys[2], (NX, NY, EZ), ((0, 8), (1, 4)), -0.2, 0.2)), 0.5, 4.0)
    gradient_map = centred(arg_keys[3], (9 * QUAD, DOF), DOF ** -0.5, 0.75, (), jnp.float32)
    trace_map = centred(arg_keys[4], (6, 6 * FACE_QUAD, DOF), DOF ** -0.5, 0.75, (), jnp.float32)
    lift_map = centred(arg_keys[5], (6, DOF, 6 * FACE_QUAD), (6 * 6 * FACE_QUAD) ** -0.5, 0.3125, (), jnp.float32)
    split_map = centred(arg_keys[6], (3 * FACE_QUAD, 3 * FACE_QUAD), (3 * FACE_QUAD) ** -0.5, 1.25, (), jnp.float32)
    spread_map = centred(arg_keys[7], (6, DOF, 3 * FACE_QUAD), (3 * FACE_QUAD) ** -0.5, 1.25, (), jnp.float32)
    fracture_faces = draw_fracture_faces(jax.random.fold_in(arg_keys[10], 71), 0)
    fracture_counts = draw_fracture_counts(jax.random.fold_in(arg_keys[10], 71), 0)
    return dict(displacement=displacement, velocity=velocity, modulus=modulus, gradient_map=gradient_map, trace_map=trace_map, lift_map=lift_map, split_map=split_map, spread_map=spread_map, fracture_faces=fracture_faces, fracture_counts=fracture_counts)


penalty = 2.0
damping = 0.5
substep = 0.1
highest = lax.Precision.HIGHEST


def face_flux(own_traces, own_rates, beside_traces, beside_rates, live_mask):
    value_rows = own_rates.shape[0]
    jump_value = beside_traces[:value_rows] - own_traces[:value_rows]
    upper_rows = penalty * jump_value + 0.5 * (beside_traces[value_rows:] + own_traces[value_rows:]) + damping * (beside_rates - own_rates)
    return jnp.concatenate([upper_rows, 0.5 * jump_value], axis=0) * live_mask


def shift_lower(values):
    return jnp.pad(values[..., :-1], ((0, 0), (0, 0), (0, 0), (1, 0)))


def shift_upper(values):
    return jnp.pad(values[..., 1:], ((0, 0), (0, 0), (0, 0), (0, 1)))


def block_force(slab_displace, slab_velocity, slab_modulus, first_plane, gradient_map, trace_map, lift_map):
    value_rows = trace_map.shape[1] // 2
    traces = jnp.einsum("fkc,cxyz->fkxyz", trace_map, slab_displace, precision=highest)
    rates = jnp.einsum("fkc,cxyz->fkxyz", trace_map[:, :value_rows], slab_velocity, precision=highest)
    centre_traces = traces[:, :, 1:-1, 1:-1]
    centre_rates = rates[:, :, 1:-1, 1:-1]
    beside_traces = [traces[1][:, :-2, 1:-1], traces[0][:, 2:, 1:-1], traces[3][:, 1:-1, :-2], traces[2][:, 1:-1, 2:], shift_lower(centre_traces[5]), shift_upper(centre_traces[4])]
    beside_rates = [rates[1][:, :-2, 1:-1], rates[0][:, 2:, 1:-1], rates[3][:, 1:-1, :-2], rates[2][:, 1:-1, 2:], shift_lower(centre_rates[5]), shift_upper(centre_rates[4])]
    grid_x = (first_plane + jnp.arange(CX, dtype=jnp.int32))[:, None, None]
    grid_y = jnp.arange(NY, dtype=jnp.int32)[None, :, None]
    grid_z = jnp.arange(EZ, dtype=jnp.int32)[None, None, :]
    shape_full = (CX, NY, EZ)
    conditions = (grid_x > 0, grid_x < NX - 1, grid_y > 0, grid_y < NY - 1, grid_z > 0, grid_z < EZ - 1)
    live_masks = [jnp.where(jnp.broadcast_to(condition, shape_full), 1.0, 0.0).astype(jnp.float32) for condition in conditions]
    fluxes = jnp.stack([face_flux(centre_traces[face_index], centre_rates[face_index], beside_traces[face_index], beside_rates[face_index], live_masks[face_index]) for face_index in range(6)])
    lifted = jnp.einsum("fck,fkxyz->cxyz", lift_map, fluxes, precision=highest)
    own_displace = slab_displace[:, 1:-1, 1:-1]
    gradients = jnp.einsum("qc,cxyz->qxyz", gradient_map, own_displace, precision=highest)
    volume = jnp.einsum("qc,qxyz->cxyz", gradient_map, gradients * slab_modulus[None], precision=highest)
    return lifted - volume


def whole_force(displace_now, velocity_now, modulus, gradient_map, trace_map, lift_map):
    padded_displace = jnp.pad(displace_now, ((0, 0), (1, 1), (1, 1), (0, 0)))
    padded_velocity = jnp.pad(velocity_now, ((0, 0), (1, 1), (1, 1), (0, 0)))

    def one_block(block_index):
        first_plane = (block_index * CX).astype(jnp.int32)
        slab_displace = lax.dynamic_slice_in_dim(padded_displace, first_plane, CX + 2, 1)
        slab_velocity = lax.dynamic_slice_in_dim(padded_velocity, first_plane, CX + 2, 1)
        slab_modulus = lax.dynamic_slice_in_dim(modulus, first_plane, CX, 0)
        return block_force(slab_displace, slab_velocity, slab_modulus, first_plane, gradient_map, trace_map, lift_map)

    blocks = lax.map(one_block, jnp.arange(N_PX, dtype=jnp.int32))
    return jnp.moveaxis(blocks, 0, 1).reshape(displace_now.shape)


def open_faces(final_displace, before, fracture_faces, fracture_counts, trace_map, split_map, spread_map):
    devices = N_PX * N_PY
    elements = CX * CY * EZ
    value_rows = 3 * FACE_QUAD
    slots = fracture_faces.shape[1]
    slot_index = jnp.broadcast_to(jnp.arange(slots, dtype=jnp.int32)[None, :], (devices, slots))
    section = jnp.where(slot_index < BLK_CAP, 0, jnp.where(slot_index < 2 * BLK_CAP, 1, 2)).astype(jnp.int32)
    offset = jnp.where(section == 0, 0, jnp.where(section == 1, BLK_CAP, 2 * BLK_CAP)).astype(jnp.int32)
    limits = jnp.take_along_axis(fracture_counts, section, axis=1)
    live_mask = jnp.where(slot_index - offset < limits, 1.0, 0.0).astype(jnp.float32).reshape(-1)
    device = jnp.broadcast_to(jnp.arange(devices, dtype=jnp.int32)[:, None], (devices, slots))
    direction = (fracture_faces // elements).reshape(-1)
    element = fracture_faces % elements
    grid_x = ((device // N_PY) * CX + element // (CY * EZ)).reshape(-1)
    grid_y = ((device % N_PY) * CY + element // EZ % CY).reshape(-1)
    grid_z = (element % EZ).reshape(-1)
    next_x = jnp.minimum(grid_x + (direction == 0).astype(jnp.int32), NX - 1)
    next_y = jnp.minimum(grid_y + (direction == 1).astype(jnp.int32), NY - 1)
    next_z = jnp.minimum(grid_z + (direction == 2).astype(jnp.int32), EZ - 1)
    own_cols = before[:, grid_x, grid_y, grid_z]
    beside_cols = before[:, next_x, next_y, next_z]
    value_map = trace_map[:, :value_rows]
    chooser = [jnp.where(direction == direction_index, 1.0, 0.0).astype(jnp.float32) for direction_index in range(3)]
    own_values = chooser[0] * jnp.dot(value_map[1], own_cols, precision=highest)
    beside_values = chooser[0] * jnp.dot(value_map[0], beside_cols, precision=highest)
    for direction_index in range(1, 3):
        own_values = own_values + chooser[direction_index] * jnp.dot(value_map[2 * direction_index + 1], own_cols, precision=highest)
        beside_values = beside_values + chooser[direction_index] * jnp.dot(value_map[2 * direction_index], beside_cols, precision=highest)
    release = jnp.dot(split_map, beside_values - own_values, precision=highest) * live_mask
    own_push = chooser[0] * jnp.dot(spread_map[1], release, precision=highest)
    beside_push = chooser[0] * jnp.dot(spread_map[0], release, precision=highest)
    for direction_index in range(1, 3):
        own_push = own_push + chooser[direction_index] * jnp.dot(spread_map[2 * direction_index + 1], release, precision=highest)
        beside_push = beside_push + chooser[direction_index] * jnp.dot(spread_map[2 * direction_index], release, precision=highest)
    result = final_displace.at[:, grid_x, grid_y, grid_z].add(-own_push)
    return result.at[:, next_x, next_y, next_z].add(beside_push)


def reference(displacement, velocity, modulus, gradient_map, trace_map, lift_map, split_map, spread_map, fracture_faces, fracture_counts):
    displace_now = displacement
    velocity_now = velocity
    before = displacement
    for subcycle in range(3):
        before = displace_now
        forces = whole_force(displace_now, velocity_now, modulus, gradient_map, trace_map, lift_map)
        velocity_now = velocity_now + substep * forces
        displace_now = displace_now + substep * velocity_now
    opened = open_faces(displace_now, before, fracture_faces, fracture_counts, trace_map, split_map, spread_map)
    return opened, velocity_now
```

```python
import jax
import jax.numpy as jnp
from jax import lax
from jax.experimental import pallas as pl
from jax.experimental.pallas import tpu as pltpu
from jax.sharding import PartitionSpec as P

BLK_CAP = 128
penalty = 2.0
damping = 0.5
substep = 0.1
F32 = jnp.float32
BF16 = jnp.bfloat16
MESH = pl.DeviceIdType.MESH


def halves(value):
    high = value.astype(BF16)
    return high, (value - high.astype(F32)).astype(BF16)


def mm(a, b):
    return jnp.dot(a, b, preferred_element_type=F32)


def kernel(
    disp_in, vel_in, mod_in, grad_in, trace_in, lift_in, split_in, spread_in, faces_in, counts_in,
    out_u, out_w, out_f,
    disp, vel, mod, grad, trace, lift, split, spread, faces, counts,
    state, state_b, wa_h, wa_l, lb_h, lb_hl, ew_hl, cb, tp, gp, lp, pp, qp, proj,
    own_h, own_l, late_h, late_l, jump_h, jump_l, leap_h, leap_l,
    send, recv, in_sem, send_sem, recv_sem,
):
    px, py = lax.axis_index("px"), lax.axis_index("py")
    nx, ny = lax.axis_size("px"), lax.axis_size("py")
    there = (px > 0, px < nx - 1, py > 0, py < ny - 1)
    beside = ({"px": px - 1}, {"px": px + 1}, {"py": py - 1}, {"py": py + 1})
    barrier = pltpu.get_barrier_semaphore()
    for side in (2, 3, 0, 1):

        @pl.when(there[side])
        def _(side=side):
            pl.semaphore_signal(barrier, inc=1, device_id=beside[side], device_id_type=MESH)

    names = ("trace", "disp", "vel", "grad", "lift", "mod", "spread", "split", "faces", "counts")
    given = (trace_in, disp_in, vel_in, grad_in, lift_in, mod_in, spread_in, split_in, faces_in, counts_in)
    local = (trace, disp, vel, grad, lift, mod, spread, split, faces, counts)
    loads = {}
    for n, name in enumerate(names):
        loads[name] = pltpu.make_async_copy(given[n], local[n], in_sem.at[n])
        loads[name].start()

    for ref in (state, tp, lp, pp, qp, gp):
        ref[...] = jnp.zeros_like(ref)
    for slot, side in ((0, 1), (1, 0), (2, 3), (3, 2)):

        @pl.when(jnp.logical_not(there[side]))
        def _(slot=slot):
            for s in range(3):
                recv[s, slot] = jnp.zeros((56, 256), F32)

    def put_a(row, value):
        high, low = halves(value)
        rows = slice(row, row + value.shape[0])
        wa_h[rows, 0:128] = high
        wa_h[rows, 128:256] = high
        wa_l[rows, :] = low

    row_id = lax.broadcasted_iota(jnp.int32, (56, 128), 0)

    def face_rows(f, sign):
        both = tp[f]
        upper = penalty * both + (sign * 0.5) * pltpu.roll(both, 29, 0)
        upper = upper + pltpu.roll(damping * both, 64, 1)
        lower = jnp.where(row_id < 54, pltpu.roll(both, 27, 0), 0.0)
        return jnp.where(row_id < 27, upper, lower)

    def put_faces(row, d, sign):
        pair = [face_rows(2 * d, sign), face_rows(2 * d + 1, sign)]
        put_a(row + 112 * d, jnp.concatenate(pair, axis=0))

    loads["trace"].wait()
    for f in range(6):
        tp[f, 0:54, 0:60] = trace[f]
    put_faces(0, 0, 1.0)
    put_faces(0, 1, 1.0)

    def block(k):
        return slice(128 * k, 128 * k + 128)

    loads["disp"].wait()
    loads["vel"].wait()
    for k in range(4):
        state[0:60, block(k)] = disp[pl.ds(k, 60, stride=4), :]
        state[64:124, block(k)] = vel[pl.ds(k, 60, stride=4), :]

    copies = [
        [
            pltpu.make_async_remote_copy(
                src_ref=send.at[s, side],
                dst_ref=recv.at[s, side],
                send_sem=send_sem.at[s, side],
                recv_sem=recv_sem.at[s, side],
                device_id=beside[side],
                device_id_type=MESH,
            )
            for side in range(4)
        ]
        for s in range(3)
    ]
    outer = ((0, 1), (2, 3), (0, 2), (1, 3))

    def split_state():
        for k in range(4):
            high, low = halves(state[:, block(k)])
            state_b[0:128, block(k)] = high
            state_b[128:256, block(k)] = low

    def project(rows):
        return mm(wa_h[rows, :], state_b[...]) + mm(wa_l[rows, :], state_b[0:128, :])

    def begin(s, d):
        for side in (2 * d, 2 * d + 1):

            @pl.when(there[side])
            def _(side=side):
                copies[s][side].start()

    split_state()
    for d in (1, 0):
        rows = slice(112 * d, 112 * d + 112)
        proj[rows, :] = project(rows)
        for f in (2 * d, 2 * d + 1):
            for half in range(2):
                send[0, f, :, block(half)] = proj[56 * f : 56 * f + 56, block(outer[f][half])]
        if d == 1:
            pl.semaphore_wait(barrier, sum(t.astype(jnp.int32) for t in there))
        begin(0, d)

    for ref in (late_h, late_l, leap_h, leap_l):
        ref[...] = jnp.zeros_like(ref)
    put_faces(0, 2, 1.0)
    for d in range(3):
        put_faces(336, d, -1.0)
    loads["grad"].wait()
    gp[0:60, 0:243] = grad[...]
    put_a(672, jnp.transpose(gp[...]))

    def put_b(column, value):
        high, low = halves(value)
        columns = slice(column, column + value.shape[1])
        lb_h[:, columns] = high
        lb_hl[0:64, columns] = high
        lb_hl[64:128, columns] = low

    put_b(384, -gp[0:64, :])
    loads["lift"].wait()
    lift_row = lax.broadcasted_iota(jnp.int32, (54, 60), 0)
    for f in range(6):
        at = 64 * (f % 2)
        lp[f // 2, at : at + 54, 0:60] = jnp.where(lift_row < 27, lift[f], 0.5 * lift[f])
    for d in range(3):
        put_b(128 * d, jnp.transpose(lp[d])[0:64, :])

    reach = []
    for f in range(4):
        rows = face_rows(f, 1.0)
        reach.append((substep * substep) * rows + substep * pltpu.roll(rows, 64, 1))
    high, low = halves(jnp.concatenate(reach, axis=0)[:, 0:64])
    carry = mm(high, lb_h[:, 0:256]) + mm(low, lb_h[:, 0:256]) + mm(high, lb_hl[64:128, 0:256])
    for i in range(2):
        pieces = [carry[112:224], carry[56 * i : 56 * i + 56], jnp.zeros((8, 256), F32)]
        cb[i] = jnp.concatenate(pieces, axis=0).astype(BF16)

    loads["spread"].wait()
    loads["split"].wait()
    qp[0:27, 0:27] = split[...]
    qp[32:59, 0:27] = split[...]
    row128 = lax.broadcasted_iota(jnp.int32, (128, 128), 0)
    placed = jnp.where(row128 < 32, pltpu.roll(qp[...], 27, 1), pltpu.roll(qp[...], 91, 1))
    for f in range(6):
        at = 32 * (f % 2)
        pp[f // 2, at : at + 27, 0:60] = spread[f]
    for d in range(3):
        part = jnp.dot(
            jnp.transpose(pp[d])[0:64, :],
            placed,
            precision=lax.Precision.HIGHEST,
            preferred_element_type=F32,
        )
        high, low = halves(-part)
        ew_hl[0:64, block(d)] = high
        ew_hl[64:128, block(d)] = low

    loads["faces"].wait()
    loads["counts"].wait()
    loads["mod"].wait()
    ids = faces[...]
    slots = lax.broadcasted_iota(jnp.int32, ids.shape, 1)
    section = jnp.where(slots < BLK_CAP, 0, jnp.where(slots < 2 * BLK_CAP, 1, 2))
    limit = jnp.where(
        section == 0,
        counts[0:1, 0:1],
        jnp.where(section == 1, BLK_CAP + counts[0:1, 1:2], 2 * BLK_CAP + counts[0:1, 2:3]),
    )
    group = jnp.where(slots < limit, ids >> 7, -1)
    spot = ids & 127
    high_hot = lax.broadcasted_iota(jnp.int32, (16, ids.shape[1]), 0) == group
    low_hot = lax.broadcasted_iota(jnp.int32, (128, ids.shape[1]), 0) == spot
    open_mask = lax.dot_general(
        high_hot.astype(F32).astype(BF16),
        low_hot.astype(F32).astype(BF16),
        (((1,), (1,)), ((), ())),
        preferred_element_type=F32,
    )

    alive = [jnp.where(t, 1.0, 0.0).astype(F32) for t in there]
    lane_row = lax.broadcasted_iota(jnp.int32, (1, 128), 1)
    not_first = (lane_row > 0).astype(F32)
    not_last = (lane_row < 127).astype(F32)

    gap = jnp.zeros((8, 128), F32)

    def put(high_ref, low_ref, row, k, value):
        high, low = halves(value)
        rows = slice(row, row + value.shape[0])
        high_ref[rows, block(k)] = high
        low_ref[rows, block(k)] = low

    def traced(f, k):
        return proj[56 * f : 56 * f + 56, block(k)]

    def own(f, k):
        return proj[336 + 56 * f : 392 + 56 * f, block(k)]

    def came(s, f, half):
        return jnp.concatenate([recv[s, f ^ 1, :, block(half)], gap], axis=0)

    def mm3(both_ref, high_ref, columns, b_high, b_low):
        both = mm(both_ref[:, columns], b_high[...])
        return both[0:64] + both[64:128] + mm(high_ref[:, columns], b_low[...])

    early, lateral = slice(0, 640), slice(0, 256)
    for s in range(3):
        if s > 0:
            for f in range(4):
                for half in range(2):
                    k = outer[f][half]
                    rest = came(s - 1, f, half) - late_h[64 * f : 64 * f + 64, block(k)].astype(F32)
                    late_l[64 * f : 64 * f + 64, block(k)] = rest.astype(BF16)
            force = mm3(lb_hl, lb_h, lateral, late_h, late_l)
            state[64:128, :] = state[64:128, :] + substep * force
            state[0:64, :] = state[0:64, :] + (substep * substep) * force
            split_state()
        todo = slice(224 if s == 0 else 0, 928)
        proj[todo, :] = project(todo)
        for k in range(4):
            i, j = k // 2, k % 2
            for d in range(3):
                n = k if d == 2 else k ^ (2 - d)
                part, jump = [], []
                for f in (2 * d, 2 * d + 1):
                    inner = d == 2 or (i, 1 - i, j, 1 - j)[f] == 1
                    if f == 4:
                        now = (pltpu.roll(traced(5, k), 1, 1) - own(4, k)) * not_first
                    elif f == 5:
                        now = (pltpu.roll(traced(4, k), 127, 1) - own(5, k)) * not_last
                    elif inner:
                        now = traced(f ^ 1, n) - own(f, k)
                    else:
                        now = own(f, k) * -alive[f]
                    part += [now, gap]
                    if s == 2:
                        if f % 2:
                            opens = open_mask[4 * d + k : 4 * d + k + 1, :]
                        elif f == 4:
                            opens = pltpu.roll(open_mask[8 + k : 9 + k, :], 1, 1)
                        elif inner:
                            opens = open_mask[4 * d + n : 4 * d + n + 1, :]
                        else:
                            half = j if d == 0 else i
                            opens = recv[1, f ^ 1, 54:55, block(half)]
                        jump += [now * opens, gap]
                put(own_h, own_l, 128 * d, k, jnp.concatenate(part, axis=0))
                if s == 2:
                    put(jump_h, jump_l, 128 * d, k, jnp.concatenate(jump, axis=0))
            put(own_h, own_l, 384, k, proj[672:928, block(k)] * mod[k : k + 1, :])
        force = mm3(lb_hl, lb_h, early, own_h, own_l)
        if s < 2:
            velocity = state[64:128, :] + substep * force
            state[64:128, :] = velocity
            state[0:64, :] = state[0:64, :] + substep * velocity
            split_state()
            ahead = project(slice(0, 224))
            for f in range(4):
                for half in range(2):
                    k = outer[f][half]
                    value = ahead[56 * f : 56 * f + 56, block(k)]
                    if s == 0 and f % 2 == 1:
                        row = 4 * (f // 2) + k
                        value = jnp.where(row_id == 54, open_mask[row : row + 1, :], value)
                    send[s + 1, f, :, block(half)] = value
        else:
            moved = state[0:64, :] + mm3(ew_hl, ew_hl.at[0:64], slice(0, 384), jump_h, jump_l)
            for k in range(4):
                out_w[pl.ds(k, 60, stride=4), :] = state[64:124, block(k)]

        for d in (0, 1):
            for side in (2 * d, 2 * d + 1):

                @pl.when(there[side])
                def _(s=s, side=side):
                    copies[s][side ^ 1].wait_recv()

            for f in (2 * d, 2 * d + 1):
                for half in range(2):
                    k = outer[f][half]
                    value = came(s, f, half)
                    if s < 2:
                        late_h[64 * f : 64 * f + 64, block(k)] = value.astype(BF16)
                    else:
                        put(late_h, late_l, 64 * f, k, value)
                        if f % 2:
                            opens = open_mask[4 * d + k : 4 * d + k + 1, :]
                        else:
                            opens = recv[1, f ^ 1, 54:55, block(half)]
                        put(leap_h, leap_l, 64 * f, k, value * opens)
        if s < 2:
            for i in range(2):
                more = mm(cb[i], late_h[:, 256 * i : 256 * i + 256])
                send[s + 1, i] = send[s + 1, i] + more[112:168]
                for f in (2, 3):
                    at = 56 * (f - 2)
                    send[s + 1, f, :, block(i)] = (
                        send[s + 1, f, :, block(i)] + more[at : at + 56, block(f - 2)]
                    )
            begin(s + 1, 1)
            begin(s + 1, 0)
        else:
            force = force + mm3(lb_hl, lb_h, lateral, late_h, late_l)
            moved = moved + mm3(ew_hl, ew_hl.at[0:64], lateral, leap_h, leap_l)
            for k in range(4):
                out_u[pl.ds(k, 60, stride=4), :] = moved[0:60, block(k)]
                out_f[pl.ds(k, 60, stride=4), :] = force[0:60, block(k)]

    for s in range(3):
        for side in range(4):

            @pl.when(there[side])
            def _(s=s, side=side):
                copies[s][side].wait_send()


def shards(
    displacement, velocity, modulus, gradient_map, trace_map, lift_map, split_map, spread_map,
    fracture_faces, fracture_counts,
):
    shape = displacement.shape
    flat = (shape[0] * 4, 128)
    args = (
        displacement.reshape(flat),
        velocity.reshape(flat),
        modulus.reshape(4, 128),
        gradient_map.T,
        trace_map,
        jnp.transpose(lift_map, (0, 2, 1)),
        split_map,
        jnp.transpose(spread_map, (0, 2, 1)),
        fracture_faces,
        fracture_counts,
    )
    vmem = pl.BlockSpec(memory_space=pltpu.VMEM)
    hbm = pl.BlockSpec(memory_space=pltpu.HBM)
    out = jax.ShapeDtypeStruct(flat, F32)
    opened, velocity_now, force = pl.pallas_call(
        kernel,
        out_shape=(out, out, out),
        in_specs=[hbm] * 10,
        out_specs=(vmem, vmem, vmem),
        scratch_shapes=[
            *(pltpu.VMEM(a.shape, a.dtype) for a in args),
            pltpu.VMEM((128, 512), F32),
            pltpu.VMEM((256, 512), BF16),
            pltpu.VMEM((928, 256), BF16),
            pltpu.VMEM((928, 128), BF16),
            pltpu.VMEM((64, 640), BF16),
            pltpu.VMEM((128, 640), BF16),
            pltpu.VMEM((128, 384), BF16),
            pltpu.VMEM((2, 176, 256), BF16),
            pltpu.VMEM((6, 56, 128), F32),
            pltpu.VMEM((128, 256), F32),
            pltpu.VMEM((3, 128, 128), F32),
            pltpu.VMEM((3, 128, 128), F32),
            pltpu.VMEM((128, 128), F32),
            pltpu.VMEM((928, 512), F32),
            pltpu.VMEM((640, 512), BF16),
            pltpu.VMEM((640, 512), BF16),
            pltpu.VMEM((256, 512), BF16),
            pltpu.VMEM((256, 512), BF16),
            pltpu.VMEM((384, 512), BF16),
            pltpu.VMEM((384, 512), BF16),
            pltpu.VMEM((256, 512), BF16),
            pltpu.VMEM((256, 512), BF16),
            pltpu.VMEM((3, 4, 56, 256), F32),
            pltpu.VMEM((3, 4, 56, 256), F32),
            pltpu.SemaphoreType.DMA((10,)),
            pltpu.SemaphoreType.DMA((3, 4)),
            pltpu.SemaphoreType.DMA((3, 4)),
        ],
        compiler_params=pltpu.CompilerParams(
            collective_id=0, has_side_effects=True, vmem_limit_bytes=40 * 1024 * 1024
        ),
    )(*(pltpu.with_memory_space_constraint(a, pltpu.HBM) for a in args))
    velocity_out = velocity_now + substep * force
    displacement_out = opened + substep * velocity_out
    return displacement_out.reshape(shape), velocity_out.reshape(shape)


def solution(mesh):
    return jax.shard_map(
        shards,
        mesh=mesh,
        in_specs=(
            P(None, "px", "py", None),
            P(None, "px", "py", None),
            P("px", "py", None),
            P(),
            P(),
            P(),
            P(),
            P(),
            P(("px", "py"), None),
            P(("px", "py"), None),
        ),
        out_specs=(P(None, "px", "py", None), P(None, "px", "py", None)),
        check_vma=False,
    )
```

```python
import functools

import jax
import jax.numpy as jnp
from jax import lax
from jax.experimental import pallas as pl
from jax.experimental.pallas import tpu as pltpu
from jax.sharding import PartitionSpec as P

BLK_CAP = 128
penalty = 2.0
damping = 0.5
substep = 0.1
F32 = jnp.float32
BF16 = jnp.bfloat16
MESH = pl.DeviceIdType.MESH


def halves(value):
    high = value.astype(BF16)
    return high, (value - high.astype(F32)).astype(BF16)


def mm(a, b):
    return jnp.dot(a, b, preferred_element_type=F32)


def kernel(
    disp_in, vel_in, mod_in, grad_in, trace_in, lift_in, split_in, spread_in, faces_in, counts_in,
    out_u, out_w, out_f,
    disp, vel, mod, grad, trace, lift, split, spread, faces, counts,
    state, state_b, wa_h, wa_l, lb_h, lb_hl, ew_hl, cb, tp, gp, lp, pp, qp, proj,
    own_h, own_l, late_h, late_l, jump_h, jump_l, leap_h, leap_l,
    send, recv, in_sem, send_sem, recv_sem,
):
    px, py = lax.axis_index("px"), lax.axis_index("py")
    nx, ny = lax.axis_size("px"), lax.axis_size("py")
    there = (px > 0, px < nx - 1, py > 0, py < ny - 1)
    beside = ({"px": px - 1}, {"px": px + 1}, {"py": py - 1}, {"py": py + 1})
    barrier = pltpu.get_barrier_semaphore()
    for side in (2, 3, 0, 1):

        @pl.when(there[side])
        def _(side=side):
            pl.semaphore_signal(barrier, inc=1, device_id=beside[side], device_id_type=MESH)

    names = ("trace", "disp", "vel", "grad", "lift", "mod", "spread", "split", "faces", "counts")
    given = (trace_in, disp_in, vel_in, grad_in, lift_in, mod_in, spread_in, split_in, faces_in, counts_in)
    local = (trace, disp, vel, grad, lift, mod, spread, split, faces, counts)
    loads = {}
    for n, name in enumerate(names):
        loads[name] = pltpu.make_async_copy(given[n], local[n], in_sem.at[0 if n < 3 else 1])
        loads[name].start()

    for ref in (state, tp, lp, pp, qp, gp):
        ref[...] = jnp.zeros_like(ref)
    for slot, side in ((0, 1), (1, 0), (2, 3), (3, 2)):

        @pl.when(jnp.logical_not(there[side]))
        def _(slot=slot):
            for s in range(3):
                recv[s, slot] = jnp.zeros((56, 256), F32)

    def put_a(row, value):
        high, low = halves(value)
        rows = slice(row, row + value.shape[0])
        wa_h[rows, 0:128] = high
        wa_h[rows, 128:256] = high
        wa_l[rows, :] = low

    row_id = lax.broadcasted_iota(jnp.int32, (56, 128), 0)

    def face_rows(f, sign):
        both = tp[f]
        upper = penalty * both + (sign * 0.5) * pltpu.roll(both, 29, 0)
        upper = upper + pltpu.roll(damping * both, 64, 1)
        lower = jnp.where(row_id < 54, pltpu.roll(both, 27, 0), 0.0)
        return jnp.where(row_id < 27, upper, lower)

    def put_faces(row, d, sign):
        pair = [face_rows(2 * d, sign), face_rows(2 * d + 1, sign)]
        put_a(row + 112 * d, jnp.concatenate(pair, axis=0))

    for name in names[:3]:
        loads[name].wait()
    for f in range(6):
        tp[f, 0:54, 0:60] = trace[f]
    put_faces(0, 0, 1.0)
    put_faces(0, 1, 1.0)

    def block(k):
        return slice(128 * k, 128 * k + 128)

    for k in range(4):
        state[0:60, block(k)] = disp[pl.ds(k, 60, stride=4), :]
        state[64:124, block(k)] = vel[pl.ds(k, 60, stride=4), :]

    copies = [
        [
            pltpu.make_async_remote_copy(
                src_ref=send.at[s, side],
                dst_ref=recv.at[s, side],
                send_sem=send_sem.at[0],
                recv_sem=recv_sem.at[s],
                device_id=beside[side],
                device_id_type=MESH,
            )
            for side in range(4)
        ]
        for s in range(3)
    ]
    sides = sum(t.astype(jnp.int32) for t in there)

    def settle(source, target, arrival, wait):
        for n in range(1, 5):
            every = pltpu.make_async_remote_copy(
                src_ref=source(n),
                dst_ref=target(n),
                send_sem=send_sem.at[0],
                recv_sem=recv_sem.at[arrival],
                device_id=beside[0],
                device_id_type=MESH,
            )
            pl.when(sides == n)(functools.partial(wait, every))

    def settle_arrivals(s):
        settle(
            lambda n: send.at[s, 0:n], lambda n: recv.at[s, 0:n], s, lambda every: every.wait_recv()
        )

    outer = ((0, 1), (2, 3), (0, 2), (1, 3))

    def split_state():
        for k in range(4):
            high, low = halves(state[:, block(k)])
            state_b[0:128, block(k)] = high
            state_b[128:256, block(k)] = low

    def project(rows):
        return mm(wa_h[rows, :], state_b[...]) + mm(wa_l[rows, :], state_b[0:128, :])

    def begin(s, d):
        for side in (2 * d, 2 * d + 1):

            @pl.when(there[side])
            def _(side=side):
                copies[s][side].start()

    split_state()
    for d in (1, 0):
        rows = slice(112 * d, 112 * d + 112)
        proj[rows, :] = project(rows)
        for f in (2 * d, 2 * d + 1):
            for half in range(2):
                send[0, f, :, block(half)] = proj[56 * f : 56 * f + 56, block(outer[f][half])]
        if d == 1:
            pl.semaphore_wait(barrier, sides)
        begin(0, d)

    for ref in (late_h, late_l, leap_h, leap_l):
        ref[...] = jnp.zeros_like(ref)
    put_faces(0, 2, 1.0)
    for d in range(3):
        put_faces(336, d, -1.0)
    for name in names[3:]:
        loads[name].wait()
    gp[0:60, 0:243] = grad[...]
    put_a(672, jnp.transpose(gp[...]))

    def put_b(column, value):
        high, low = halves(value)
        columns = slice(column, column + value.shape[1])
        lb_h[:, columns] = high
        lb_hl[0:64, columns] = high
        lb_hl[64:128, columns] = low

    put_b(384, -gp[0:64, :])
    lift_row = lax.broadcasted_iota(jnp.int32, (54, 60), 0)
    for f in range(6):
        at = 64 * (f % 2)
        lp[f // 2, at : at + 54, 0:60] = jnp.where(lift_row < 27, lift[f], 0.5 * lift[f])
    for d in range(3):
        put_b(128 * d, jnp.transpose(lp[d])[0:64, :])

    reach = []
    for f in range(4):
        rows = face_rows(f, 1.0)
        reach.append((substep * substep) * rows + substep * pltpu.roll(rows, 64, 1))
    high, low = halves(jnp.concatenate(reach, axis=0)[:, 0:64])
    carry = mm(high, lb_h[:, 0:256]) + mm(low, lb_h[:, 0:256]) + mm(high, lb_hl[64:128, 0:256])
    for i in range(2):
        pieces = [carry[112:224], carry[56 * i : 56 * i + 56], jnp.zeros((8, 256), F32)]
        cb[i] = jnp.concatenate(pieces, axis=0).astype(BF16)

    qp[0:27, 0:27] = split[...]
    qp[32:59, 0:27] = split[...]
    row128 = lax.broadcasted_iota(jnp.int32, (128, 128), 0)
    placed = jnp.where(row128 < 32, pltpu.roll(qp[...], 27, 1), pltpu.roll(qp[...], 91, 1))
    for f in range(6):
        at = 32 * (f % 2)
        pp[f // 2, at : at + 27, 0:60] = spread[f]
    for d in range(3):
        part = jnp.dot(
            jnp.transpose(pp[d])[0:64, :],
            placed,
            precision=lax.Precision.HIGHEST,
            preferred_element_type=F32,
        )
        high, low = halves(-part)
        ew_hl[0:64, block(d)] = high
        ew_hl[64:128, block(d)] = low

    ids = faces[...]
    slots = lax.broadcasted_iota(jnp.int32, ids.shape, 1)
    section = jnp.where(slots < BLK_CAP, 0, jnp.where(slots < 2 * BLK_CAP, 1, 2))
    limit = jnp.where(
        section == 0,
        counts[0:1, 0:1],
        jnp.where(section == 1, BLK_CAP + counts[0:1, 1:2], 2 * BLK_CAP + counts[0:1, 2:3]),
    )
    group = jnp.where(slots < limit, ids >> 7, -1)
    spot = ids & 127
    high_hot = lax.broadcasted_iota(jnp.int32, (16, ids.shape[1]), 0) == group
    low_hot = lax.broadcasted_iota(jnp.int32, (128, ids.shape[1]), 0) == spot
    open_mask = lax.dot_general(
        high_hot.astype(F32).astype(BF16),
        low_hot.astype(F32).astype(BF16),
        (((1,), (1,)), ((), ())),
        preferred_element_type=F32,
    )

    alive = [jnp.where(t, 1.0, 0.0).astype(F32) for t in there]
    lane_row = lax.broadcasted_iota(jnp.int32, (1, 128), 1)
    not_first = (lane_row > 0).astype(F32)
    not_last = (lane_row < 127).astype(F32)

    gap = jnp.zeros((8, 128), F32)

    def put(high_ref, low_ref, row, k, value):
        high, low = halves(value)
        rows = slice(row, row + value.shape[0])
        high_ref[rows, block(k)] = high
        low_ref[rows, block(k)] = low

    def traced(f, k):
        return proj[56 * f : 56 * f + 56, block(k)]

    def own(f, k):
        return proj[336 + 56 * f : 392 + 56 * f, block(k)]

    def came(s, f, half):
        return jnp.concatenate([recv[s, f ^ 1, :, block(half)], gap], axis=0)

    def mm3(both_ref, high_ref, columns, b_high, b_low):
        both = mm(both_ref[:, columns], b_high[...])
        return both[0:64] + both[64:128] + mm(high_ref[:, columns], b_low[...])

    early, lateral = slice(0, 640), slice(0, 256)
    for s in range(3):
        if s > 0:
            for f in range(4):
                for half in range(2):
                    k = outer[f][half]
                    rest = came(s - 1, f, half) - late_h[64 * f : 64 * f + 64, block(k)].astype(F32)
                    late_l[64 * f : 64 * f + 64, block(k)] = rest.astype(BF16)
            force = mm3(lb_hl, lb_h, lateral, late_h, late_l)
            state[64:128, :] = state[64:128, :] + substep * force
            state[0:64, :] = state[0:64, :] + (substep * substep) * force
            split_state()
        todo = slice(224 if s == 0 else 0, 928)
        proj[todo, :] = project(todo)
        for k in range(4):
            i, j = k // 2, k % 2
            for d in range(3):
                n = k if d == 2 else k ^ (2 - d)
                part, jump = [], []
                for f in (2 * d, 2 * d + 1):
                    inner = d == 2 or (i, 1 - i, j, 1 - j)[f] == 1
                    if f == 4:
                        now = (pltpu.roll(traced(5, k), 1, 1) - own(4, k)) * not_first
                    elif f == 5:
                        now = (pltpu.roll(traced(4, k), 127, 1) - own(5, k)) * not_last
                    elif inner:
                        now = traced(f ^ 1, n) - own(f, k)
                    else:
                        now = own(f, k) * -alive[f]
                    part += [now, gap]
                    if s == 2:
                        if f % 2:
                            opens = open_mask[4 * d + k : 4 * d + k + 1, :]
                        elif f == 4:
                            opens = pltpu.roll(open_mask[8 + k : 9 + k, :], 1, 1)
                        elif inner:
                            opens = open_mask[4 * d + n : 4 * d + n + 1, :]
                        else:
                            half = j if d == 0 else i
                            opens = recv[1, f ^ 1, 54:55, block(half)]
                        jump += [now * opens, gap]
                put(own_h, own_l, 128 * d, k, jnp.concatenate(part, axis=0))
                if s == 2:
                    put(jump_h, jump_l, 128 * d, k, jnp.concatenate(jump, axis=0))
            put(own_h, own_l, 384, k, proj[672:928, block(k)] * mod[k : k + 1, :])
        force = mm3(lb_hl, lb_h, early, own_h, own_l)
        if s < 2:
            velocity = state[64:128, :] + substep * force
            state[64:128, :] = velocity
            state[0:64, :] = state[0:64, :] + substep * velocity
            split_state()
            ahead = project(slice(0, 224))
            for f in range(4):
                for half in range(2):
                    k = outer[f][half]
                    value = ahead[56 * f : 56 * f + 56, block(k)]
                    if s == 0 and f % 2 == 1:
                        row = 4 * (f // 2) + k
                        value = jnp.where(row_id == 54, open_mask[row : row + 1, :], value)
                    send[s + 1, f, :, block(half)] = value
        else:
            moved = state[0:64, :] + mm3(ew_hl, ew_hl.at[0:64], slice(0, 384), jump_h, jump_l)
            for k in range(4):
                out_w[pl.ds(k, 60, stride=4), :] = state[64:124, block(k)]

        settle_arrivals(s)
        for d in (0, 1):
            for f in (2 * d, 2 * d + 1):
                for half in range(2):
                    k = outer[f][half]
                    value = came(s, f, half)
                    if s < 2:
                        late_h[64 * f : 64 * f + 64, block(k)] = value.astype(BF16)
                    else:
                        put(late_h, late_l, 64 * f, k, value)
                        if f % 2:
                            opens = open_mask[4 * d + k : 4 * d + k + 1, :]
                        else:
                            opens = recv[1, f ^ 1, 54:55, block(half)]
                        put(leap_h, leap_l, 64 * f, k, value * opens)
        if s < 2:
            for i in range(2):
                more = mm(cb[i], late_h[:, 256 * i : 256 * i + 256])
                send[s + 1, i] = send[s + 1, i] + more[112:168]
                for f in (2, 3):
                    at = 56 * (f - 2)
                    send[s + 1, f, :, block(i)] = (
                        send[s + 1, f, :, block(i)] + more[at : at + 56, block(f - 2)]
                    )
            begin(s + 1, 1)
            begin(s + 1, 0)
        else:
            force = force + mm3(lb_hl, lb_h, lateral, late_h, late_l)
            moved = moved + mm3(ew_hl, ew_hl.at[0:64], lateral, leap_h, leap_l)
            for k in range(4):
                out_u[pl.ds(k, 60, stride=4), :] = moved[0:60, block(k)]
                out_f[pl.ds(k, 60, stride=4), :] = force[0:60, block(k)]

    settle(
        lambda n: send.at[:, 0:n], lambda n: recv.at[:, 0:n], 0, lambda every: every.wait_send()
    )


def shards(
    displacement, velocity, modulus, gradient_map, trace_map, lift_map, split_map, spread_map,
    fracture_faces, fracture_counts,
):
    shape = displacement.shape
    flat = (shape[0] * 4, 128)
    args = (
        displacement.reshape(flat),
        velocity.reshape(flat),
        modulus.reshape(4, 128),
        gradient_map.T,
        trace_map,
        jnp.transpose(lift_map, (0, 2, 1)),
        split_map,
        jnp.transpose(spread_map, (0, 2, 1)),
        fracture_faces,
        fracture_counts,
    )
    vmem = pl.BlockSpec(memory_space=pltpu.VMEM)
    hbm = pl.BlockSpec(memory_space=pltpu.HBM)
    out = jax.ShapeDtypeStruct(flat, F32)
    opened, velocity_now, force = pl.pallas_call(
        kernel,
        out_shape=(out, out, out),
        in_specs=[hbm] * 10,
        out_specs=(vmem, vmem, vmem),
        scratch_shapes=[
            *(pltpu.VMEM(a.shape, a.dtype) for a in args),
            pltpu.VMEM((128, 512), F32),
            pltpu.VMEM((256, 512), BF16),
            pltpu.VMEM((928, 256), BF16),
            pltpu.VMEM((928, 128), BF16),
            pltpu.VMEM((64, 640), BF16),
            pltpu.VMEM((128, 640), BF16),
            pltpu.VMEM((128, 384), BF16),
            pltpu.VMEM((2, 176, 256), BF16),
            pltpu.VMEM((6, 56, 128), F32),
            pltpu.VMEM((128, 256), F32),
            pltpu.VMEM((3, 128, 128), F32),
            pltpu.VMEM((3, 128, 128), F32),
            pltpu.VMEM((128, 128), F32),
            pltpu.VMEM((928, 512), F32),
            pltpu.VMEM((640, 512), BF16),
            pltpu.VMEM((640, 512), BF16),
            pltpu.VMEM((256, 512), BF16),
            pltpu.VMEM((256, 512), BF16),
            pltpu.VMEM((384, 512), BF16),
            pltpu.VMEM((384, 512), BF16),
            pltpu.VMEM((256, 512), BF16),
            pltpu.VMEM((256, 512), BF16),
            pltpu.VMEM((3, 4, 56, 256), F32),
            pltpu.VMEM((3, 4, 56, 256), F32),
            pltpu.SemaphoreType.DMA((2,)),
            pltpu.SemaphoreType.DMA((1,)),
            pltpu.SemaphoreType.DMA((3,)),
        ],
        compiler_params=pltpu.CompilerParams(
            collective_id=0, has_side_effects=True, vmem_limit_bytes=40 * 1024 * 1024
        ),
    )(*(pltpu.with_memory_space_constraint(a, pltpu.HBM) for a in args))
    velocity_out = velocity_now + substep * force
    displacement_out = opened + substep * velocity_out
    return displacement_out.reshape(shape), velocity_out.reshape(shape)


def solution(mesh):
    return jax.shard_map(
        shards,
        mesh=mesh,
        in_specs=(
            P(None, "px", "py", None),
            P(None, "px", "py", None),
            P("px", "py", None),
            P(),
            P(),
            P(),
            P(),
            P(),
            P(("px", "py"), None),
            P(("px", "py"), None),
        ),
        out_specs=(P(None, "px", "py", None), P(None, "px", "py", None)),
        check_vma=False,
    )
```

```python
import jax
import jax.numpy as jnp
from jax import lax
from jax.experimental import pallas as pl
from jax.experimental.pallas import tpu as pltpu
from jax.sharding import PartitionSpec as P

BLK_CAP = 128
penalty = 2.0
damping = 0.5
substep = 0.1
F32 = jnp.float32
BF16 = jnp.bfloat16
MESH = pl.DeviceIdType.MESH


def halves(value):
    high = value.astype(BF16)
    return high, (value - high.astype(F32)).astype(BF16)


def mm(a, b):
    return jnp.dot(a, b, preferred_element_type=F32)


def kernel(
    disp_in, vel_in, mod_in, grad_in, trace_in, lift_in, split_in, spread_in, faces_in, counts_in,
    out_u, out_w, out_f,
    disp, vel, mod, grad, trace, lift, split, spread, faces, counts,
    state, state_b, wa_h, wa_l, lb_h, lb_hl, ew_hl, cy, cx, cn, known, near, tp, gp, lp, pp, qp, proj,
    own_h, own_l, late_h, late_l, jump_h, jump_l, leap_h, leap_l,
    send, recv, in_sem, send_sem, recv_sem,
):
    px, py = lax.axis_index("px"), lax.axis_index("py")
    nx, ny = lax.axis_size("px"), lax.axis_size("py")
    odd = px % 2
    across, partner = px - 1 + 2 * odd, px + 1 - 2 * odd
    there = (
        jnp.logical_and(across >= 0, across < nx), partner >= 0, py > 0, py < ny - 1,
    )
    beside = ({"px": across}, {"px": partner}, {"py": py - 1}, {"py": py + 1})
    barrier = pltpu.get_barrier_semaphore()
    for side in (2, 3, 0, 1):

        @pl.when(there[side])
        def _(side=side):
            pl.semaphore_signal(barrier, inc=1, device_id=beside[side], device_id_type=MESH)

    def placed_face(f):
        return f + odd - 2 * f * odd if f < 2 else f

    def either(if_odd, if_even):
        return jnp.where(odd == 1, if_odd, if_even)

    names = ("trace", "disp", "vel", "grad", "lift", "mod", "spread", "split", "faces", "counts")
    given = (trace_in, disp_in, vel_in, grad_in, lift_in, mod_in, spread_in, split_in, faces_in, counts_in)
    local = (trace, disp, vel, grad, lift, mod, spread, split, faces, counts)
    loads = {}
    for n, name in enumerate(names):
        loads[name] = pltpu.make_async_copy(given[n], local[n], in_sem.at[0 if n < 3 else 1])
        loads[name].start()

    for ref in (state, tp, lp, pp, qp, gp):
        ref[...] = jnp.zeros_like(ref)
    for f in range(4):

        @pl.when(jnp.logical_not(there[f]))
        def _(f=f):
            for base in (0, 4, 8):
                recv[base + f] = jnp.zeros((56, 256), F32)

    def put_a(row, value):
        high, low = halves(value)
        rows = slice(row, row + value.shape[0])
        wa_h[rows, 0:128] = high
        wa_h[rows, 128:256] = high
        wa_l[rows, :] = low

    row_id = lax.broadcasted_iota(jnp.int32, (56, 128), 0)

    def face_rows(f, sign):
        both = tp[f]
        upper = penalty * both + (sign * 0.5) * pltpu.roll(both, 29, 0)
        upper = upper + pltpu.roll(damping * both, 64, 1)
        lower = jnp.where(row_id < 54, pltpu.roll(both, 27, 0), 0.0)
        return jnp.where(row_id < 27, upper, lower)

    def put_faces(row, d, sign):
        pair = [face_rows(2 * d, sign), face_rows(2 * d + 1, sign)]
        put_a(row + 112 * d, jnp.concatenate(pair, axis=0))

    for name in names[:3]:
        loads[name].wait()
    for f in range(6):
        tp[f, 0:54, 0:60] = trace[placed_face(f)]
    put_faces(0, 0, 1.0)
    put_faces(0, 1, 1.0)

    def block(k):
        return slice(128 * k, 128 * k + 128)

    for k in range(4):
        for row, ref in ((0, disp), (64, vel)):
            state[row : row + 60, block(k)] = either(
                ref[pl.ds(k ^ 2, 60, stride=4), :], ref[pl.ds(k, 60, stride=4), :]
            )

    def faced(f):
        return f if f < 2 else f ^ 1

    copies = [
        pltpu.make_async_remote_copy(
            src_ref=send.at[slot],
            dst_ref=recv.at[slot - slot % 4 + faced(slot % 4)],
            send_sem=send_sem.at[0],
            recv_sem=recv_sem.at[slot // 2],
            device_id=beside[slot % 4],
            device_id_type=MESH,
        )
        for slot in range(12)
    ]

    def begin(*slots):
        for slot in slots:
            pl.when(there[slot % 4])(copies[slot].start)

    def settle(pair):
        first = there[pair % 2 * 2].astype(jnp.int32)
        both = first + there[pair % 2 * 2 + 1].astype(jnp.int32)
        for n in (1, 2):
            every = pltpu.make_async_remote_copy(
                src_ref=send.at[0:n],
                dst_ref=recv.at[0:n],
                send_sem=send_sem.at[0],
                recv_sem=recv_sem.at[pair],
                device_id=beside[1],
                device_id_type=MESH,
            )
            pl.when(both == n)(every.wait_recv)

    outer = ((0, 1), (2, 3), (0, 2), (1, 3))

    def split_state():
        for k in range(4):
            high, low = halves(state[:, block(k)])
            state_b[0:128, block(k)] = high
            state_b[128:256, block(k)] = low

    def project(rows):
        return mm(wa_h[rows, :], state_b[...]) + mm(wa_l[rows, :], state_b[0:128, :])

    split_state()
    for d in (1, 0):
        rows = slice(112 * d, 112 * d + 112)
        proj[rows, :] = project(rows)
        for f in (2 * d, 2 * d + 1):
            for half in range(2):
                send[f, :, block(half)] = proj[56 * f : 56 * f + 56, block(outer[f][half])]
        if d == 1:
            pl.semaphore_wait(barrier, sum(t.astype(jnp.int32) for t in there))
        begin(2 * d, 2 * d + 1)
    for ref in (late_h, late_l, leap_h, leap_l):
        ref[...] = jnp.zeros_like(ref)
    put_faces(0, 2, 1.0)
    for d in range(3):
        put_faces(336, d, -1.0)
    for name in names[3:]:
        loads[name].wait()
    gp[0:60, 0:243] = grad[...]
    put_a(672, jnp.transpose(gp[...]))

    def put_b(column, value):
        high, low = halves(value)
        columns = slice(column, column + value.shape[1])
        lb_h[:, columns] = high
        lb_hl[0:64, columns] = high
        lb_hl[64:128, columns] = low

    put_b(384, -gp[0:64, :])
    lift_row = lax.broadcasted_iota(jnp.int32, (54, 60), 0)
    for f in range(6):
        at = 64 * (f % 2)
        lp[f // 2, at : at + 54, 0:60] = jnp.where(
            lift_row < 27, lift[placed_face(f)], 0.5 * lift[placed_face(f)]
        )
    for d in range(3):
        put_b(128 * d, jnp.transpose(lp[d])[0:64, :])

    reach = []
    for f in range(4):
        rows = face_rows(f, 1.0)
        reach.append((substep * substep) * rows + substep * pltpu.roll(rows, 64, 1))
    high, low = halves(jnp.concatenate(reach, axis=0)[:, 0:64])
    carry = mm(high, lb_h[:, 0:256]) + mm(low, lb_h[:, 0:256]) + mm(high, lb_hl[64:128, 0:256])
    cy[...] = carry[112:224, 0:128].astype(BF16)
    cx[...] = carry[0:112, 128:256].astype(BF16)
    for f in range(4):
        o = f ^ 1
        pieces = [carry[56 * o : 56 * o + 56, 64 * o : 64 * o + 64], jnp.zeros((8, 64), F32)]
        cn[f] = jnp.concatenate(pieces, axis=0).astype(BF16)

    qp[0:27, 0:27] = split[...]
    qp[32:59, 0:27] = split[...]
    row128 = lax.broadcasted_iota(jnp.int32, (128, 128), 0)
    placed = jnp.where(row128 < 32, pltpu.roll(qp[...], 27, 1), pltpu.roll(qp[...], 91, 1))
    for f in range(6):
        at = 32 * (f % 2)
        pp[f // 2, at : at + 27, 0:60] = spread[placed_face(f)]
    for d in range(3):
        part = jnp.dot(
            jnp.transpose(pp[d])[0:64, :],
            placed,
            precision=lax.Precision.HIGHEST,
            preferred_element_type=F32,
        )
        high, low = halves(-part)
        ew_hl[0:64, block(d)] = high
        ew_hl[64:128, block(d)] = low

    ids = faces[...]
    slots = lax.broadcasted_iota(jnp.int32, ids.shape, 1)
    section = jnp.where(slots < BLK_CAP, 0, jnp.where(slots < 2 * BLK_CAP, 1, 2))
    limit = jnp.where(
        section == 0,
        counts[0:1, 0:1],
        jnp.where(section == 1, BLK_CAP + counts[0:1, 1:2], 2 * BLK_CAP + counts[0:1, 2:3]),
    )
    group = ids >> 7
    group = jnp.where(group < 4, group, (group & 12) + ((group + 2 * odd) & 3))
    group = jnp.where(slots < limit, group, -1)
    spot = ids & 127
    high_hot = lax.broadcasted_iota(jnp.int32, (16, ids.shape[1]), 0) == group
    low_hot = lax.broadcasted_iota(jnp.int32, (128, ids.shape[1]), 0) == spot
    open_mask = lax.dot_general(
        high_hot.astype(F32).astype(BF16),
        low_hot.astype(F32).astype(BF16),
        (((1,), (1,)), ((), ())),
        preferred_element_type=F32,
    )

    alive = [jnp.where(t, 1.0, 0.0).astype(F32) for t in there]
    lane_row = lax.broadcasted_iota(jnp.int32, (1, 128), 1)
    not_first = (lane_row > 0).astype(F32)
    not_last = (lane_row < 127).astype(F32)

    gap = jnp.zeros((8, 128), F32)

    def put(high_ref, low_ref, row, k, value):
        high, low = halves(value)
        rows = slice(row, row + value.shape[0])
        high_ref[rows, block(k)] = high
        low_ref[rows, block(k)] = low

    def traced(f, k):
        return proj[56 * f : 56 * f + 56, block(k)]

    def own(f, k):
        return proj[336 + 56 * f : 392 + 56 * f, block(k)]

    def came(s, f, half):
        value = recv[4 * s + f, :, block(half)]
        if s > 0:
            value = value + known[f, 0:56, block(half)]
        return jnp.concatenate([value, gap], axis=0)

    def arrive(s, f):
        for half in range(2):
            value = came(s, f, half)
            late_h[64 * f : 64 * f + 64, block(outer[f][half])] = value.astype(BF16)

    def opens(f, k):
        i, j = k // 2, k % 2
        n = k if f > 3 else k ^ (2 - f // 2)
        inner = f > 3 or (i, 1 - i, j, 1 - j)[f] == 1
        if f == 4:
            return pltpu.roll(open_mask[8 + k : 9 + k, :], 1, 1)
        if f in (3, 5):
            row = 4 * (f // 2) + k
            return open_mask[row : row + 1, :]
        if f == 2:
            return open_mask[4 + n : 5 + n, :] if inner else recv[6, 54:55, block(i)]
        if inner:
            return open_mask[j : j + 1, :]
        mine, other = open_mask[2 + j : 3 + j, :], recv[4 + f, 54:55, block(j)]
        return either(mine, other) if f == 0 else either(other, mine)

    def mm3(both_ref, high_ref, columns, b_high, b_low):
        both = mm(both_ref[:, columns], b_high[...])
        return both[0:64] + both[64:128] + mm(high_ref[:, columns], b_low[...])

    early, lateral = slice(0, 640), slice(0, 256)
    moduli = [either(mod[k ^ 2 : (k ^ 2) + 1, :], mod[k : k + 1, :]) for k in range(4)]
    for s in range(3):
        if s > 0:
            for f in range(4):
                for half in range(2):
                    k = outer[f][half]
                    rest = came(s - 1, f, half) - late_h[64 * f : 64 * f + 64, block(k)].astype(F32)
                    late_l[64 * f : 64 * f + 64, block(k)] = rest.astype(BF16)
            force = mm3(lb_hl, lb_h, lateral, late_h, late_l)
            state[64:128, :] = state[64:128, :] + substep * force
            state[0:64, :] = state[0:64, :] + (substep * substep) * force
            split_state()
            for f in range(4):
                for half in range(2):
                    value = traced(f, outer[f][half]) * alive[f]
                    near[f, :, block(half)] = jnp.concatenate([value, gap], axis=0).astype(BF16)
                known[f] = mm(cn[f], near[f])
        todo = slice(224 if s == 0 else 0, 928)
        proj[todo, :] = project(todo)
        for k in range(4):
            i, j = k // 2, k % 2
            for d in range(3):
                n = k if d == 2 else k ^ (2 - d)
                part, jump = [], []
                for f in (2 * d, 2 * d + 1):
                    inner = d == 2 or (i, 1 - i, j, 1 - j)[f] == 1
                    if f == 4:
                        now = (pltpu.roll(traced(5, k), 1, 1) - own(4, k)) * not_first
                    elif f == 5:
                        now = (pltpu.roll(traced(4, k), 127, 1) - own(5, k)) * not_last
                    elif inner:
                        now = traced(f ^ 1, n) - own(f, k)
                    else:
                        now = own(f, k) * -alive[f]
                    part += [now, gap]
                    if s == 2:
                        jump += [now * opens(f, k), gap]
                put(own_h, own_l, 128 * d, k, jnp.concatenate(part, axis=0))
                if s == 2:
                    put(jump_h, jump_l, 128 * d, k, jnp.concatenate(jump, axis=0))
            put(own_h, own_l, 384, k, proj[672:928, block(k)] * moduli[k])
        force = mm3(lb_hl, lb_h, early, own_h, own_l)
        if s < 2:
            velocity = state[64:128, :] + substep * force
            state[64:128, :] = velocity
            state[0:64, :] = state[0:64, :] + substep * velocity
            split_state()
            ahead = project(slice(0, 224))
            for f in range(4):
                for half in range(2):
                    k = outer[f][half]
                    value = ahead[56 * f : 56 * f + 56, block(k)]
                    if s == 0 and f != 2:
                        row = 4 + k if f == 3 else 2 + half
                        value = jnp.where(row_id == 54, open_mask[row : row + 1, :], value)
                    send[4 * s + 4 + f, :, block(half)] = value
        else:
            moved = state[0:64, :] + mm3(ew_hl, ew_hl.at[0:64], slice(0, 384), jump_h, jump_l)
            for k in range(4):
                out_w[pl.ds(k, 60, stride=4), :] = either(
                    state[64:124, block(k ^ 2)], state[64:124, block(k)]
                )

        if s < 2:
            then = 4 * s + 4
            settle(2 * s)
            for f in (1, 0):
                arrive(s, f)
            more = mm(cy[...], late_h[0:128, :])
            for f in (2, 3):
                at = 56 * (f - 2)
                for half in range(2):
                    send[then + f, :, block(half)] = (
                        send[then + f, :, block(half)] + more[at : at + 56, block(outer[f][half])]
                    )
            begin(then + 2, then + 3)
            settle(2 * s + 1)
            for f in (2, 3):
                arrive(s, f)
            more = mm(cx[...], late_h[128:256, :])
            for f in (0, 1):
                at = 56 * f
                send[then + f] = send[then + f] + more[at : at + 56, 256 * f : 256 * f + 256]
            begin(then, then + 1)
        else:
            settle(4)
            settle(5)
            for f in range(4):
                for half in range(2):
                    k = outer[f][half]
                    value = came(2, f, half)
                    put(late_h, late_l, 64 * f, k, value)
                    put(leap_h, leap_l, 64 * f, k, value * opens(f, k))
            force = force + mm3(lb_hl, lb_h, lateral, late_h, late_l)
            moved = moved + mm3(ew_hl, ew_hl.at[0:64], lateral, leap_h, leap_l)
            for k in range(4):
                out_u[pl.ds(k, 60, stride=4), :] = either(
                    moved[0:60, block(k ^ 2)], moved[0:60, block(k)]
                )
                out_f[pl.ds(k, 60, stride=4), :] = either(
                    force[0:60, block(k ^ 2)], force[0:60, block(k)]
                )

    for n in range(1, 5):
        every = pltpu.make_async_remote_copy(
            src_ref=send.at[0 : 3 * n],
            dst_ref=recv.at[0 : 3 * n],
            send_sem=send_sem.at[0],
            recv_sem=recv_sem.at[0],
            device_id=beside[1],
            device_id_type=MESH,
        )
        pl.when(sum(t.astype(jnp.int32) for t in there) == n)(every.wait_send)


def shards(
    displacement, velocity, modulus, gradient_map, trace_map, lift_map, split_map, spread_map,
    fracture_faces, fracture_counts,
):
    shape = displacement.shape
    flat = (shape[0] * 4, 128)
    args = (
        displacement.reshape(flat),
        velocity.reshape(flat),
        modulus.reshape(4, 128),
        gradient_map.T,
        trace_map,
        jnp.transpose(lift_map, (0, 2, 1)),
        split_map,
        jnp.transpose(spread_map, (0, 2, 1)),
        fracture_faces,
        fracture_counts,
    )
    vmem = pl.BlockSpec(memory_space=pltpu.VMEM)
    hbm = pl.BlockSpec(memory_space=pltpu.HBM)
    out = jax.ShapeDtypeStruct(flat, F32)
    opened, velocity_now, force = pl.pallas_call(
        kernel,
        out_shape=(out, out, out),
        in_specs=[hbm] * 10,
        out_specs=(vmem, vmem, vmem),
        scratch_shapes=[
            *(pltpu.VMEM(a.shape, a.dtype) for a in args),
            pltpu.VMEM((128, 512), F32),
            pltpu.VMEM((256, 512), BF16),
            pltpu.VMEM((928, 256), BF16),
            pltpu.VMEM((928, 128), BF16),
            pltpu.VMEM((64, 640), BF16),
            pltpu.VMEM((128, 640), BF16),
            pltpu.VMEM((128, 384), BF16),
            pltpu.VMEM((112, 128), BF16),
            pltpu.VMEM((112, 128), BF16),
            pltpu.VMEM((4, 64, 64), BF16),
            pltpu.VMEM((4, 64, 256), F32),
            pltpu.VMEM((4, 64, 256), BF16),
            pltpu.VMEM((6, 56, 128), F32),
            pltpu.VMEM((128, 256), F32),
            pltpu.VMEM((3, 128, 128), F32),
            pltpu.VMEM((3, 128, 128), F32),
            pltpu.VMEM((128, 128), F32),
            pltpu.VMEM((928, 512), F32),
            pltpu.VMEM((640, 512), BF16),
            pltpu.VMEM((640, 512), BF16),
            pltpu.VMEM((256, 512), BF16),
            pltpu.VMEM((256, 512), BF16),
            pltpu.VMEM((384, 512), BF16),
            pltpu.VMEM((384, 512), BF16),
            pltpu.VMEM((256, 512), BF16),
            pltpu.VMEM((256, 512), BF16),
            pltpu.VMEM((12, 56, 256), F32),
            pltpu.VMEM((12, 56, 256), F32),
            pltpu.SemaphoreType.DMA((2,)),
            pltpu.SemaphoreType.DMA((1,)),
            pltpu.SemaphoreType.DMA((6,)),
        ],
        compiler_params=pltpu.CompilerParams(
            collective_id=0, has_side_effects=True, vmem_limit_bytes=40 * 1024 * 1024
        ),
    )(*(pltpu.with_memory_space_constraint(a, pltpu.HBM) for a in args))
    velocity_out = velocity_now + substep * force
    displacement_out = opened + substep * velocity_out
    return displacement_out.reshape(shape), velocity_out.reshape(shape)


def solution(mesh):
    return jax.shard_map(
        shards,
        mesh=mesh,
        in_specs=(
            P(None, "px", "py", None),
            P(None, "px", "py", None),
            P("px", "py", None),
            P(),
            P(),
            P(),
            P(),
            P(),
            P(("px", "py"), None),
            P(("px", "py"), None),
        ),
        out_specs=(P(None, "px", "py", None), P(None, "px", "py", None)),
        check_vma=False,
    )
```

```python
import jax
import jax.numpy as jnp
from jax import lax
from jax.experimental import pallas as pl
from jax.experimental.pallas import tpu as pltpu
from jax.sharding import PartitionSpec as P

BLK_CAP = 128
penalty = 2.0
damping = 0.5
substep = 0.1
F32 = jnp.float32
BF16 = jnp.bfloat16
MESH = pl.DeviceIdType.MESH


def halves(value):
    high = value.astype(BF16)
    return high, (value - high.astype(F32)).astype(BF16)


def mm(a, b):
    return jnp.dot(a, b, preferred_element_type=F32)


def kernel(
    disp_in, vel_in, mod_in, grad_in, trace_in, lift_in, split_in, spread_in, faces_in, counts_in,
    out_u, out_w, out_f,
    disp, vel, mod, grad, trace, lift, split, spread, faces, counts,
    state, state_b, wa_h, wa_l, lb_h, lb_hl, ew_hl, cy, cx, cn, known, near, tp, gp, lp, pp, qp, proj,
    own_h, own_l, late_h, late_l, jump_h, jump_l, leap_h, leap_l,
    send, recv, in_sem, send_sem, recv_sem,
):
    px, py = lax.axis_index("px"), lax.axis_index("py")
    nx, ny = lax.axis_size("px"), lax.axis_size("py")
    odd = px % 2
    across, partner = px - 1 + 2 * odd, px + 1 - 2 * odd
    there = (
        jnp.logical_and(across >= 0, across < nx), partner >= 0, py > 0, py < ny - 1,
    )
    beside = ({"px": across}, {"px": partner}, {"py": py - 1}, {"py": py + 1})
    barrier = pltpu.get_barrier_semaphore()
    for side in (2, 3, 0, 1):

        @pl.when(there[side])
        def _(side=side):
            pl.semaphore_signal(barrier, inc=1, device_id=beside[side], device_id_type=MESH)

    def placed_face(f):
        return f + odd - 2 * f * odd if f < 2 else f

    def either(if_odd, if_even):
        return jnp.where(odd == 1, if_odd, if_even)

    names = ("trace", "disp", "vel", "grad", "lift", "mod", "spread", "split", "faces", "counts")
    given = (trace_in, disp_in, vel_in, grad_in, lift_in, mod_in, spread_in, split_in, faces_in, counts_in)
    local = (trace, disp, vel, grad, lift, mod, spread, split, faces, counts)
    loads = {}
    for n, name in enumerate(names):
        loads[name] = pltpu.make_async_copy(given[n], local[n], in_sem.at[0 if n < 3 else 1])
        loads[name].start()

    for ref in (state, tp, lp, pp, qp, gp):
        ref[...] = jnp.zeros_like(ref)
    for f in range(4):

        @pl.when(jnp.logical_not(there[f]))
        def _(f=f):
            for base in (0, 4, 8):
                recv[base + f] = jnp.zeros((56, 256), F32)

    def put_a(row, value):
        high, low = halves(value)
        rows = slice(row, row + value.shape[0])
        wa_h[rows, 0:128] = high
        wa_h[rows, 128:256] = high
        wa_l[rows, :] = low

    row_id = lax.broadcasted_iota(jnp.int32, (56, 128), 0)

    def face_rows(f, sign):
        both = tp[f]
        upper = penalty * both + (sign * 0.5) * pltpu.roll(both, 29, 0)
        upper = upper + pltpu.roll(damping * both, 64, 1)
        lower = jnp.where(row_id < 54, pltpu.roll(both, 27, 0), 0.0)
        return jnp.where(row_id < 27, upper, lower)

    def put_faces(row, d, sign):
        pair = [face_rows(2 * d, sign), face_rows(2 * d + 1, sign)]
        put_a(row + 112 * d, jnp.concatenate(pair, axis=0))

    for name in names[:3]:
        loads[name].wait()
    for f in range(6):
        tp[f, 0:54, 0:60] = trace[placed_face(f)]
    put_faces(0, 0, 1.0)
    put_faces(0, 1, 1.0)

    def block(k):
        return slice(128 * k, 128 * k + 128)

    for k in range(4):
        for row, ref in ((0, disp), (64, vel)):
            state[row : row + 60, block(k)] = either(
                ref[pl.ds(k ^ 2, 60, stride=4), :], ref[pl.ds(k, 60, stride=4), :]
            )

    def faced(f):
        return f if f < 2 else f ^ 1

    def copy(slot, columns=slice(0, 256)):
        return pltpu.make_async_remote_copy(
            src_ref=send.at[slot, :, columns],
            dst_ref=recv.at[slot - slot % 4 + faced(slot % 4), :, columns],
            send_sem=send_sem.at[0],
            recv_sem=recv_sem.at[slot // 4, (0, 1, 2, 2)[slot % 4]],
            device_id=beside[slot % 4],
            device_id_type=MESH,
        )

    def begin(*slots, columns=slice(0, 256)):
        for slot in slots:
            pl.when(there[slot % 4])(copy(slot, columns).start)

    def settle_x(s, f):
        pl.when(there[f])(copy(4 * s + f).wait_recv)

    def settle_y(s):
        both = there[2].astype(jnp.int32) + there[3].astype(jnp.int32)
        for n in (1, 2):
            every = pltpu.make_async_remote_copy(
                src_ref=send.at[0:n],
                dst_ref=recv.at[0:n],
                send_sem=send_sem.at[0],
                recv_sem=recv_sem.at[s, 2],
                device_id=beside[1],
                device_id_type=MESH,
            )
            pl.when(both == n)(every.wait_recv)

    outer = ((0, 1), (2, 3), (0, 2), (1, 3))

    def split_state():
        for k in range(4):
            high, low = halves(state[:, block(k)])
            state_b[0:128, block(k)] = high
            state_b[128:256, block(k)] = low

    def project(rows):
        return mm(wa_h[rows, :], state_b[...]) + mm(wa_l[rows, :], state_b[0:128, :])

    split_state()
    for d in (1, 0):
        rows = slice(112 * d, 112 * d + 112)
        proj[rows, :] = project(rows)
        for f in (2 * d, 2 * d + 1):
            for half in range(2):
                send[f, :, block(half)] = proj[56 * f : 56 * f + 56, block(outer[f][half])]
        if d == 1:
            pl.semaphore_wait(barrier, sum(t.astype(jnp.int32) for t in there))
        begin(2 * d, 2 * d + 1)
    for ref in (late_h, late_l, leap_h, leap_l):
        ref[...] = jnp.zeros_like(ref)
    put_faces(0, 2, 1.0)
    for d in range(3):
        put_faces(336, d, -1.0)
    for name in names[3:]:
        loads[name].wait()
    gp[0:60, 0:243] = grad[...]
    put_a(672, jnp.transpose(gp[...]))

    def put_b(column, value):
        high, low = halves(value)
        columns = slice(column, column + value.shape[1])
        lb_h[:, columns] = high
        lb_hl[0:64, columns] = high
        lb_hl[64:128, columns] = low

    put_b(384, -gp[0:64, :])
    lift_row = lax.broadcasted_iota(jnp.int32, (54, 60), 0)
    for f in range(6):
        at = 64 * (f % 2)
        lp[f // 2, at : at + 54, 0:60] = jnp.where(
            lift_row < 27, lift[placed_face(f)], 0.5 * lift[placed_face(f)]
        )
    for d in range(3):
        put_b(128 * d, jnp.transpose(lp[d])[0:64, :])

    reach = []
    for f in range(4):
        rows = face_rows(f, 1.0)
        reach.append((substep * substep) * rows + substep * pltpu.roll(rows, 64, 1))
    high, low = halves(jnp.concatenate(reach, axis=0)[:, 0:64])
    carry = mm(high, lb_h[:, 0:256]) + mm(low, lb_h[:, 0:256]) + mm(high, lb_hl[64:128, 0:256])
    cy[...] = carry[112:224, 0:128].astype(BF16)
    cx[...] = carry[0:112, 128:256].astype(BF16)
    for f in range(4):
        o = f ^ 1
        pieces = [carry[56 * o : 56 * o + 56, 64 * o : 64 * o + 64], jnp.zeros((8, 64), F32)]
        cn[f] = jnp.concatenate(pieces, axis=0).astype(BF16)

    qp[0:27, 0:27] = split[...]
    qp[32:59, 0:27] = split[...]
    row128 = lax.broadcasted_iota(jnp.int32, (128, 128), 0)
    placed = jnp.where(row128 < 32, pltpu.roll(qp[...], 27, 1), pltpu.roll(qp[...], 91, 1))
    for f in range(6):
        at = 32 * (f % 2)
        pp[f // 2, at : at + 27, 0:60] = spread[placed_face(f)]
    for d in range(3):
        part = jnp.dot(
            jnp.transpose(pp[d])[0:64, :],
            placed,
            precision=lax.Precision.HIGHEST,
            preferred_element_type=F32,
        )
        high, low = halves(-part)
        ew_hl[0:64, block(d)] = high
        ew_hl[64:128, block(d)] = low

    ids = faces[...]
    slots = lax.broadcasted_iota(jnp.int32, ids.shape, 1)
    section = jnp.where(slots < BLK_CAP, 0, jnp.where(slots < 2 * BLK_CAP, 1, 2))
    limit = jnp.where(
        section == 0,
        counts[0:1, 0:1],
        jnp.where(section == 1, BLK_CAP + counts[0:1, 1:2], 2 * BLK_CAP + counts[0:1, 2:3]),
    )
    group = ids >> 7
    group = jnp.where(group < 4, group, (group & 12) + ((group + 2 * odd) & 3))
    group = jnp.where(slots < limit, group, -1)
    spot = ids & 127
    high_hot = lax.broadcasted_iota(jnp.int32, (16, ids.shape[1]), 0) == group
    low_hot = lax.broadcasted_iota(jnp.int32, (128, ids.shape[1]), 0) == spot
    open_mask = lax.dot_general(
        high_hot.astype(F32).astype(BF16),
        low_hot.astype(F32).astype(BF16),
        (((1,), (1,)), ((), ())),
        preferred_element_type=F32,
    )

    alive = [jnp.where(t, 1.0, 0.0).astype(F32) for t in there]
    lane_row = lax.broadcasted_iota(jnp.int32, (1, 128), 1)
    not_first = (lane_row > 0).astype(F32)
    not_last = (lane_row < 127).astype(F32)

    gap = jnp.zeros((8, 128), F32)

    def put(high_ref, low_ref, row, k, value):
        high, low = halves(value)
        rows = slice(row, row + value.shape[0])
        high_ref[rows, block(k)] = high
        low_ref[rows, block(k)] = low

    def traced(f, k):
        return proj[56 * f : 56 * f + 56, block(k)]

    def own(f, k):
        return proj[336 + 56 * f : 392 + 56 * f, block(k)]

    def came(s, f, half):
        value = recv[4 * s + f, :, block(half)]
        if s > 0:
            value = value + known[f, 0:56, block(half)]
        return jnp.concatenate([value, gap], axis=0)

    def arrive(s, f):
        for half in range(2):
            value = came(s, f, half)
            late_h[64 * f : 64 * f + 64, block(outer[f][half])] = value.astype(BF16)

    def opens(f, k):
        i, j = k // 2, k % 2
        n = k if f > 3 else k ^ (2 - f // 2)
        inner = f > 3 or (i, 1 - i, j, 1 - j)[f] == 1
        if f == 4:
            return pltpu.roll(open_mask[8 + k : 9 + k, :], 1, 1)
        if f in (3, 5):
            row = 4 * (f // 2) + k
            return open_mask[row : row + 1, :]
        if f == 2:
            return open_mask[4 + n : 5 + n, :] if inner else recv[6, 54:55, block(i)]
        if inner:
            return open_mask[j : j + 1, :]
        mine, other = open_mask[2 + j : 3 + j, :], recv[4 + f, 54:55, block(j)]
        return either(mine, other) if f == 0 else either(other, mine)

    def mm3(both_ref, high_ref, columns, b_high, b_low):
        both = mm(both_ref[:, columns], b_high[...])
        return both[0:64] + both[64:128] + mm(high_ref[:, columns], b_low[...])

    early, lateral = slice(0, 640), slice(0, 256)
    moduli = [either(mod[k ^ 2 : (k ^ 2) + 1, :], mod[k : k + 1, :]) for k in range(4)]
    for s in range(3):
        if s > 0:
            for f in range(4):
                for half in range(2):
                    k = outer[f][half]
                    rest = came(s - 1, f, half) - late_h[64 * f : 64 * f + 64, block(k)].astype(F32)
                    late_l[64 * f : 64 * f + 64, block(k)] = rest.astype(BF16)
            force = mm3(lb_hl, lb_h, lateral, late_h, late_l)
            state[64:128, :] = state[64:128, :] + substep * force
            state[0:64, :] = state[0:64, :] + (substep * substep) * force
            split_state()
            for f in range(4):
                for half in range(2):
                    value = traced(f, outer[f][half]) * alive[f]
                    near[f, :, block(half)] = jnp.concatenate([value, gap], axis=0).astype(BF16)
                known[f] = mm(cn[f], near[f])
        todo = slice(224 if s == 0 else 0, 928)
        proj[todo, :] = project(todo)
        for k in range(4):
            i, j = k // 2, k % 2
            for d in range(3):
                n = k if d == 2 else k ^ (2 - d)
                part, jump = [], []
                for f in (2 * d, 2 * d + 1):
                    inner = d == 2 or (i, 1 - i, j, 1 - j)[f] == 1
                    if f == 4:
                        now = (pltpu.roll(traced(5, k), 1, 1) - own(4, k)) * not_first
                    elif f == 5:
                        now = (pltpu.roll(traced(4, k), 127, 1) - own(5, k)) * not_last
                    elif inner:
                        now = traced(f ^ 1, n) - own(f, k)
                    else:
                        now = own(f, k) * -alive[f]
                    part += [now, gap]
                    if s == 2:
                        jump += [now * opens(f, k), gap]
                put(own_h, own_l, 128 * d, k, jnp.concatenate(part, axis=0))
                if s == 2:
                    put(jump_h, jump_l, 128 * d, k, jnp.concatenate(jump, axis=0))
            put(own_h, own_l, 384, k, proj[672:928, block(k)] * moduli[k])
        force = mm3(lb_hl, lb_h, early, own_h, own_l)
        if s < 2:
            velocity = state[64:128, :] + substep * force
            state[64:128, :] = velocity
            state[0:64, :] = state[0:64, :] + substep * velocity
            split_state()
            ahead = project(slice(0, 224))
            for f in range(4):
                for half in range(2):
                    k = outer[f][half]
                    value = ahead[56 * f : 56 * f + 56, block(k)]
                    if s == 0 and f != 2:
                        row = 4 + k if f == 3 else 2 + half
                        value = jnp.where(row_id == 54, open_mask[row : row + 1, :], value)
                    send[4 * s + 4 + f, :, block(half)] = value
        else:
            moved = state[0:64, :] + mm3(ew_hl, ew_hl.at[0:64], slice(0, 384), jump_h, jump_l)
            for k in range(4):
                out_w[pl.ds(k, 60, stride=4), :] = either(
                    state[64:124, block(k ^ 2)], state[64:124, block(k)]
                )

        if s < 2:
            then = 4 * s + 4
            def after_x(f, s=s, then=then):
                settle_x(s, f)
                arrive(s, f)
                more = mm(cy[...], late_h[0:128, 256 * f : 256 * f + 256])
                for y in (2, 3):
                    at = 56 * (y - 2)
                    send[then + y, :, block(f)] = (
                        send[then + y, :, block(f)] + more[at : at + 56, block(y - 2)]
                    )
                begin(then + 2, then + 3, columns=block(f))

            def after_y(s=s, then=then):
                settle_y(s)
                for f in (2, 3):
                    arrive(s, f)
                more = mm(cx[...], late_h[128:256, :])
                for f in (0, 1):
                    at = 56 * f
                    send[then + f] = send[then + f] + more[at : at + 56, 256 * f : 256 * f + 256]
                begin(then, then + 1)

            after_x(1)

            @pl.when(odd == 0)
            def _():
                after_x(0)
                after_y()

            @pl.when(odd == 1)
            def _():
                after_y()
                after_x(0)

        else:
            settle_x(2, 1)
            settle_y(2)
            settle_x(2, 0)
            for f in range(4):
                for half in range(2):
                    k = outer[f][half]
                    value = came(2, f, half)
                    put(late_h, late_l, 64 * f, k, value)
                    put(leap_h, leap_l, 64 * f, k, value * opens(f, k))
            force = force + mm3(lb_hl, lb_h, lateral, late_h, late_l)
            moved = moved + mm3(ew_hl, ew_hl.at[0:64], lateral, leap_h, leap_l)
            for k in range(4):
                out_u[pl.ds(k, 60, stride=4), :] = either(
                    moved[0:60, block(k ^ 2)], moved[0:60, block(k)]
                )
                out_f[pl.ds(k, 60, stride=4), :] = either(
                    force[0:60, block(k ^ 2)], force[0:60, block(k)]
                )

    for n in range(1, 5):
        every = pltpu.make_async_remote_copy(
            src_ref=send.at[0 : 3 * n],
            dst_ref=recv.at[0 : 3 * n],
            send_sem=send_sem.at[0],
            recv_sem=recv_sem.at[0, 0],
            device_id=beside[1],
            device_id_type=MESH,
        )
        pl.when(sum(t.astype(jnp.int32) for t in there) == n)(every.wait_send)


def shards(
    displacement, velocity, modulus, gradient_map, trace_map, lift_map, split_map, spread_map,
    fracture_faces, fracture_counts,
):
    shape = displacement.shape
    flat = (shape[0] * 4, 128)
    args = (
        displacement.reshape(flat),
        velocity.reshape(flat),
        modulus.reshape(4, 128),
        gradient_map.T,
        trace_map,
        jnp.transpose(lift_map, (0, 2, 1)),
        split_map,
        jnp.transpose(spread_map, (0, 2, 1)),
        fracture_faces,
        fracture_counts,
    )
    vmem = pl.BlockSpec(memory_space=pltpu.VMEM)
    hbm = pl.BlockSpec(memory_space=pltpu.HBM)
    out = jax.ShapeDtypeStruct(flat, F32)
    opened, velocity_now, force = pl.pallas_call(
        kernel,
        out_shape=(out, out, out),
        in_specs=[hbm] * 10,
        out_specs=(vmem, vmem, vmem),
        scratch_shapes=[
            *(pltpu.VMEM(a.shape, a.dtype) for a in args),
            pltpu.VMEM((128, 512), F32),
            pltpu.VMEM((256, 512), BF16),
            pltpu.VMEM((928, 256), BF16),
            pltpu.VMEM((928, 128), BF16),
            pltpu.VMEM((64, 640), BF16),
            pltpu.VMEM((128, 640), BF16),
            pltpu.VMEM((128, 384), BF16),
            pltpu.VMEM((112, 128), BF16),
            pltpu.VMEM((112, 128), BF16),
            pltpu.VMEM((4, 64, 64), BF16),
            pltpu.VMEM((4, 64, 256), F32),
            pltpu.VMEM((4, 64, 256), BF16),
            pltpu.VMEM((6, 56, 128), F32),
            pltpu.VMEM((128, 256), F32),
            pltpu.VMEM((3, 128, 128), F32),
            pltpu.VMEM((3, 128, 128), F32),
            pltpu.VMEM((128, 128), F32),
            pltpu.VMEM((928, 512), F32),
            pltpu.VMEM((640, 512), BF16),
            pltpu.VMEM((640, 512), BF16),
            pltpu.VMEM((256, 512), BF16),
            pltpu.VMEM((256, 512), BF16),
            pltpu.VMEM((384, 512), BF16),
            pltpu.VMEM((384, 512), BF16),
            pltpu.VMEM((256, 512), BF16),
            pltpu.VMEM((256, 512), BF16),
            pltpu.VMEM((12, 56, 256), F32),
            pltpu.VMEM((12, 56, 256), F32),
            pltpu.SemaphoreType.DMA((2,)),
            pltpu.SemaphoreType.DMA((1,)),
            pltpu.SemaphoreType.DMA((3, 3)),
        ],
        compiler_params=pltpu.CompilerParams(
            collective_id=0, has_side_effects=True, vmem_limit_bytes=40 * 1024 * 1024
        ),
    )(*(pltpu.with_memory_space_constraint(a, pltpu.HBM) for a in args))
    velocity_out = velocity_now + substep * force
    displacement_out = opened + substep * velocity_out
    return displacement_out.reshape(shape), velocity_out.reshape(shape)


def solution(mesh):
    return jax.shard_map(
        shards,
        mesh=mesh,
        in_specs=(
            P(None, "px", "py", None),
            P(None, "px", "py", None),
            P("px", "py", None),
            P(),
            P(),
            P(),
            P(),
            P(),
            P(("px", "py"), None),
            P(("px", "py"), None),
        ),
        out_specs=(P(None, "px", "py", None), P(None, "px", "py", None)),
        check_vma=False,
    )
```

```python
import jax
import jax.numpy as jnp
from jax import lax
from jax.experimental import pallas as pl
from jax.experimental.pallas import tpu as pltpu
from jax.sharding import PartitionSpec as P

BLK_CAP = 128
penalty = 2.0
damping = 0.5
substep = 0.1
F32 = jnp.float32
BF16 = jnp.bfloat16
MESH = pl.DeviceIdType.MESH


def halves(value):
    high = value.astype(BF16)
    return high, (value - high.astype(F32)).astype(BF16)


def mm(a, b):
    return jnp.dot(a, b, preferred_element_type=F32)


def kernel(
    disp_in, vel_in, mod_in, grad_in, trace_in, lift_in, split_in, spread_in, faces_in, counts_in,
    out_u, out_w, out_f,
    disp, vel, mod, grad, trace, lift, split, spread, faces, counts,
    state, state_b, wa_h, wa_l, lb_h, lb_hl, ew_hl, cy, cx, cn, known, near, tp, gp, lp, pp, qp, proj,
    own_h, own_l, late_h, late_l, jump_h, jump_l, leap, e2,
    send, recv, in_sem, send_sem, recv_sem,
):
    px, py = lax.axis_index("px"), lax.axis_index("py")
    nx, ny = lax.axis_size("px"), lax.axis_size("py")
    odd = px % 2
    across, partner = px - 1 + 2 * odd, px + 1 - 2 * odd
    there = (
        jnp.logical_and(across >= 0, across < nx), partner >= 0, py > 0, py < ny - 1,
    )
    beside = ({"px": across}, {"px": partner}, {"py": py - 1}, {"py": py + 1})
    barrier = pltpu.get_barrier_semaphore()
    for side in (2, 3, 0, 1):

        @pl.when(there[side])
        def _(side=side):
            pl.semaphore_signal(barrier, inc=1, device_id=beside[side], device_id_type=MESH)

    def placed_face(f):
        return f + odd - 2 * f * odd if f < 2 else f

    def either(if_odd, if_even):
        return jnp.where(odd == 1, if_odd, if_even)

    names = ("trace", "disp", "vel", "grad", "lift", "mod", "spread", "split", "faces", "counts")
    given = (trace_in, disp_in, vel_in, grad_in, lift_in, mod_in, spread_in, split_in, faces_in, counts_in)
    local = (trace, disp, vel, grad, lift, mod, spread, split, faces, counts)
    loads = {}
    for n, name in enumerate(names):
        loads[name] = pltpu.make_async_copy(given[n], local[n], in_sem.at[0])
        if n < 3:
            loads[name].start()

    for ref in (state, tp, lp, pp, qp, gp):
        ref[...] = jnp.zeros_like(ref)
    for f in range(4):

        @pl.when(jnp.logical_not(there[f]))
        def _(f=f):
            for base in (0, 4, 8):
                recv[base + f] = jnp.zeros((56, 256), F32)

    def put_a(row, value):
        high, low = halves(value)
        rows = slice(row, row + value.shape[0])
        wa_h[rows, 0:128] = high
        wa_h[rows, 128:256] = high
        wa_l[rows, :] = low

    row_id = lax.broadcasted_iota(jnp.int32, (56, 128), 0)

    def face_rows(f, sign):
        both = tp[f]
        upper = penalty * both + (sign * 0.5) * pltpu.roll(both, 29, 0)
        upper = upper + pltpu.roll(damping * both, 64, 1)
        lower = jnp.where(row_id < 54, pltpu.roll(both, 27, 0), 0.0)
        return jnp.where(row_id < 27, upper, lower)

    def put_faces(row, d, sign):
        pair = [face_rows(2 * d, sign), face_rows(2 * d + 1, sign)]
        put_a(row + 112 * d, jnp.concatenate(pair, axis=0))

    for name in names[:3]:
        loads[name].wait()
    for name in names[3:]:
        loads[name].start()
    for f in range(6):
        tp[f, 0:54, 0:60] = trace[placed_face(f)]
    put_faces(0, 0, 1.0)
    put_faces(0, 1, 1.0)

    def block(k):
        return slice(128 * k, 128 * k + 128)

    for k in range(4):
        for row, ref in ((0, disp), (64, vel)):
            state[row : row + 60, block(k)] = either(
                ref[pl.ds(k ^ 2, 60, stride=4), :], ref[pl.ds(k, 60, stride=4), :]
            )

    def faced(f):
        return f if f < 2 else f ^ 1

    def copy(slot, columns=slice(0, 256)):
        return pltpu.make_async_remote_copy(
            src_ref=send.at[slot, :, columns],
            dst_ref=recv.at[slot - slot % 4 + faced(slot % 4), :, columns],
            send_sem=send_sem.at[0],
            recv_sem=recv_sem.at[min(slot // 4 * 3 + (0, 1, 2, 2)[slot % 4], 6)],
            device_id=beside[slot % 4],
            device_id_type=MESH,
        )

    def begin(*slots, columns=slice(0, 256)):
        for slot in slots:
            pl.when(there[slot % 4])(copy(slot, columns).start)

    def settle_x(s, f):
        pl.when(there[f])(copy(4 * s + f).wait_recv)

    def settle_y(s):
        both = there[2].astype(jnp.int32) + there[3].astype(jnp.int32)
        for n in (1, 2):
            every = pltpu.make_async_remote_copy(
                src_ref=send.at[0:n],
                dst_ref=recv.at[0:n],
                send_sem=send_sem.at[0],
                recv_sem=recv_sem.at[3 * s + 2],
                device_id=beside[1],
                device_id_type=MESH,
            )
            pl.when(both == n)(every.wait_recv)

    outer = ((0, 1), (2, 3), (0, 2), (1, 3))

    def split_state():
        for k in range(4):
            high, low = halves(state[:, block(k)])
            state_b[0:128, block(k)] = high
            state_b[128:256, block(k)] = low

    def project(rows):
        return mm(wa_h[rows, :], state_b[...]) + mm(wa_l[rows, :], state_b[0:128, :])

    split_state()
    proj[0:224, :] = project(slice(0, 224))
    for f in range(4):
        for half in range(2):
            send[f, :, block(half)] = proj[56 * f : 56 * f + 56, block(outer[f][half])]
    pl.semaphore_wait(barrier, sum(t.astype(jnp.int32) for t in there))
    begin(0, 2, 3, 1)

    for ref in (late_h, late_l, leap):
        ref[...] = jnp.zeros_like(ref)
    put_faces(0, 2, 1.0)
    for d in range(3):
        put_faces(336, d, -1.0)
    for name in names[3:]:
        loads[name].wait()
    gp[0:60, 0:243] = grad[...]
    put_a(672, jnp.transpose(gp[...]))

    def put_b(column, value):
        high, low = halves(value)
        columns = slice(column, column + value.shape[1])
        lb_h[:, columns] = high
        lb_hl[0:64, columns] = high
        lb_hl[64:128, columns] = low

    put_b(384, -gp[0:64, :])
    lift_row = lax.broadcasted_iota(jnp.int32, (54, 60), 0)
    for f in range(6):
        at = 64 * (f % 2)
        lp[f // 2, at : at + 54, 0:60] = jnp.where(
            lift_row < 27, lift[placed_face(f)], 0.5 * lift[placed_face(f)]
        )
    for d in range(3):
        put_b(128 * d, jnp.transpose(lp[d])[0:64, :])

    reach = []
    for f in range(4):
        rows = face_rows(f, 1.0)
        reach.append((substep * substep) * rows + substep * pltpu.roll(rows, 64, 1))
    high, low = halves(jnp.concatenate(reach, axis=0)[:, 0:64])
    carry = mm(high, lb_h[:, 0:256]) + mm(low, lb_h[:, 0:256]) + mm(high, lb_hl[64:128, 0:256])
    cy[...] = carry[112:224, 0:128].astype(BF16)
    cx[...] = carry[0:112, 128:256].astype(BF16)
    for f in range(4):
        o = f ^ 1
        pieces = [carry[56 * o : 56 * o + 56, 64 * o : 64 * o + 64], jnp.zeros((8, 64), F32)]
        cn[f] = jnp.concatenate(pieces, axis=0).astype(BF16)

    qp[0:27, 0:27] = split[...]
    qp[32:59, 0:27] = split[...]
    row128 = lax.broadcasted_iota(jnp.int32, (128, 128), 0)
    placed = jnp.where(row128 < 32, pltpu.roll(qp[...], 27, 1), pltpu.roll(qp[...], 91, 1))
    for f in range(6):
        at = 32 * (f % 2)
        pp[f // 2, at : at + 27, 0:60] = spread[placed_face(f)]
    lane64 = lax.broadcasted_iota(jnp.int32, (64, 128), 1)
    packed = jnp.zeros((64, 128), F32)
    for d in range(3):
        part = jnp.dot(
            jnp.transpose(pp[d])[0:64, :],
            placed,
            precision=lax.Precision.HIGHEST,
            preferred_element_type=F32,
        )
        high, low = halves(-part)
        ew_hl[0:64, block(d)] = high
        ew_hl[64:128, block(d)] = low
        if d < 2:
            first = jnp.where(lane64 < 64, -part, 0.0)
            packed += pltpu.roll(first, (104, 40)[d], 1)
            packed += pltpu.roll(-part - first, (72, 8)[d], 1)
    high, low = halves(packed)
    e2[0:64, 0:128] = high
    e2[0:64, 128:256] = high
    e2[64:128, 0:128] = low
    e2[64:128, 128:256] = jnp.zeros((64, 128), BF16)

    ids = faces[...]
    slots = lax.broadcasted_iota(jnp.int32, ids.shape, 1)
    section = jnp.where(slots < BLK_CAP, 0, jnp.where(slots < 2 * BLK_CAP, 1, 2))
    limit = jnp.where(
        section == 0,
        counts[0:1, 0:1],
        jnp.where(section == 1, BLK_CAP + counts[0:1, 1:2], 2 * BLK_CAP + counts[0:1, 2:3]),
    )
    group = ids >> 7
    group = jnp.where(group < 4, group, (group & 12) + ((group + 2 * odd) & 3))
    group = jnp.where(slots < limit, group, -1)
    spot = ids & 127
    high_hot = lax.broadcasted_iota(jnp.int32, (16, ids.shape[1]), 0) == group
    low_hot = lax.broadcasted_iota(jnp.int32, (128, ids.shape[1]), 0) == spot
    open_mask = lax.dot_general(
        high_hot.astype(F32).astype(BF16),
        low_hot.astype(F32).astype(BF16),
        (((1,), (1,)), ((), ())),
        preferred_element_type=F32,
    )

    alive = [jnp.where(t, 1.0, 0.0).astype(F32) for t in there]
    lane_row = lax.broadcasted_iota(jnp.int32, (1, 128), 1)
    not_first = (lane_row > 0).astype(F32)
    not_last = (lane_row < 127).astype(F32)

    gap = jnp.zeros((8, 128), F32)

    def put(high_ref, low_ref, row, k, value):
        high, low = halves(value)
        rows = slice(row, row + value.shape[0])
        high_ref[rows, block(k)] = high
        low_ref[rows, block(k)] = low

    def traced(f, k):
        return proj[56 * f : 56 * f + 56, block(k)]

    def own(f, k):
        return proj[336 + 56 * f : 392 + 56 * f, block(k)]

    def came(s, f, half):
        value = recv[4 * s + f, :, block(half)]
        if s > 0:
            value = value + known[f, 0:56, block(half)]
        return jnp.concatenate([value, gap], axis=0)

    def arrive(s, f):
        for half in range(2):
            value = came(s, f, half)
            late_h[64 * f : 64 * f + 64, block(outer[f][half])] = value.astype(BF16)

    def opens(f, k):
        i, j = k // 2, k % 2
        n = k if f > 3 else k ^ (2 - f // 2)
        inner = f > 3 or (i, 1 - i, j, 1 - j)[f] == 1
        if f == 4:
            return pltpu.roll(open_mask[8 + k : 9 + k, :], 1, 1)
        if f in (3, 5):
            row = 4 * (f // 2) + k
            return open_mask[row : row + 1, :]
        if f == 2:
            return open_mask[4 + n : 5 + n, :] if inner else recv[6, 54:55, block(i)]
        if inner:
            return open_mask[j : j + 1, :]
        mine, other = open_mask[2 + j : 3 + j, :], recv[4 + f, 54:55, block(j)]
        return either(mine, other) if f == 0 else either(other, mine)

    def mm3(both_ref, high_ref, columns, b_high, b_low):
        both = mm(both_ref[:, columns], b_high[...])
        return both[0:64] + both[64:128] + mm(high_ref[:, columns], b_low[...])

    early, lateral = slice(0, 640), slice(0, 256)
    moduli = [either(mod[k ^ 2 : (k ^ 2) + 1, :], mod[k : k + 1, :]) for k in range(4)]
    for s in range(3):
        if s > 0:
            for f in range(4):
                for half in range(2):
                    k = outer[f][half]
                    rest = came(s - 1, f, half) - late_h[64 * f : 64 * f + 64, block(k)].astype(F32)
                    late_l[64 * f : 64 * f + 64, block(k)] = rest.astype(BF16)
            force = mm3(lb_hl, lb_h, lateral, late_h, late_l)
            state[64:128, :] = state[64:128, :] + substep * force
            state[0:64, :] = state[0:64, :] + (substep * substep) * force
            split_state()
            for f in range(4):
                for half in range(2):
                    value = traced(f, outer[f][half]) * alive[f]
                    near[f, :, block(half)] = jnp.concatenate([value, gap], axis=0).astype(BF16)
                known[f] = mm(cn[f], near[f])
        todo = slice(224 if s == 0 else 0, 928)
        proj[todo, :] = project(todo)
        for k in range(4):
            i, j = k // 2, k % 2
            for d in range(3):
                n = k if d == 2 else k ^ (2 - d)
                part, jump = [], []
                for f in (2 * d, 2 * d + 1):
                    inner = d == 2 or (i, 1 - i, j, 1 - j)[f] == 1
                    if f == 4:
                        now = (pltpu.roll(traced(5, k), 1, 1) - own(4, k)) * not_first
                    elif f == 5:
                        now = (pltpu.roll(traced(4, k), 127, 1) - own(5, k)) * not_last
                    elif inner:
                        now = traced(f ^ 1, n) - own(f, k)
                    else:
                        now = own(f, k) * -alive[f]
                    part += [now, gap]
                    if s == 2:
                        jump += [now * opens(f, k), gap]
                put(own_h, own_l, 128 * d, k, jnp.concatenate(part, axis=0))
                if s == 2:
                    put(jump_h, jump_l, 128 * d, k, jnp.concatenate(jump, axis=0))
            put(own_h, own_l, 384, k, proj[672:928, block(k)] * moduli[k])
        force = mm3(lb_hl, lb_h, early, own_h, own_l)
        if s < 2:
            velocity = state[64:128, :] + substep * force
            state[64:128, :] = velocity
            state[0:64, :] = state[0:64, :] + substep * velocity
            split_state()
            ahead = project(slice(0, 224))
            for f in range(4):
                for half in range(2):
                    k = outer[f][half]
                    value = ahead[56 * f : 56 * f + 56, block(k)]
                    if s == 0 and f != 2:
                        row = 4 + k if f == 3 else 2 + half
                        value = jnp.where(row_id == 54, open_mask[row : row + 1, :], value)
                    send[4 * s + 4 + f, :, block(half)] = value
        else:
            moved = state[0:64, :] + mm3(ew_hl, ew_hl.at[0:64], slice(0, 384), jump_h, jump_l)
            for k in range(4):
                out_w[pl.ds(k, 60, stride=4), :] = either(
                    state[64:124, block(k ^ 2)], state[64:124, block(k)]
                )

        if s < 2:
            then = 4 * s + 4
            def after_x(f, s=s, then=then):
                settle_x(s, f)
                arrive(s, f)
                more = mm(cy[...], late_h[0:128, 256 * f : 256 * f + 256])
                for y in (2, 3):
                    at = 56 * (y - 2)
                    send[then + y, :, block(f)] = (
                        send[then + y, :, block(f)] + more[at : at + 56, block(y - 2)]
                    )
                begin(then + 2, then + 3, columns=block(f))

            def after_y(s=s, then=then):
                settle_y(s)
                for f in (2, 3):
                    arrive(s, f)
                more = mm(cx[...], late_h[128:256, :])
                for f in (0, 1):
                    at = 56 * f
                    send[then + f] = send[then + f] + more[at : at + 56, 256 * f : 256 * f + 256]
                begin(then, then + 1)

            after_x(1)

            @pl.when(odd == 0)
            def _():
                after_x(0)
                after_y()

            @pl.when(odd == 1)
            def _():
                after_y()
                after_x(0)

        else:
            every_side = sum(t.astype(jnp.int32) for t in there)
            for n in range(1, 5):
                every = pltpu.make_async_remote_copy(
                    src_ref=send.at[0:n],
                    dst_ref=recv.at[0:n],
                    send_sem=send_sem.at[0],
                    recv_sem=recv_sem.at[6],
                    device_id=beside[1],
                    device_id_type=MESH,
                )
                pl.when(every_side == n)(every.wait_recv)
            for f in range(4):
                for half in range(2):
                    k = outer[f][half]
                    value = came(2, f, half)
                    put(late_h, late_l, 64 * f, k, value)
                    high, low = halves(value[24:56] * opens(f, k))
                    leap[32 * f : 32 * f + 32, block(k)] = high
                    leap[128 + 32 * f : 160 + 32 * f, block(k)] = low
            force = force + mm3(lb_hl, lb_h, lateral, late_h, late_l)
            both = mm(e2[...], leap[...])
            moved = moved + both[0:64] + both[64:128]
            for k in range(4):
                out_u[pl.ds(k, 60, stride=4), :] = either(
                    moved[0:60, block(k ^ 2)], moved[0:60, block(k)]
                )
                out_f[pl.ds(k, 60, stride=4), :] = either(
                    force[0:60, block(k ^ 2)], force[0:60, block(k)]
                )

    for n in range(1, 5):
        every = pltpu.make_async_remote_copy(
            src_ref=send.at[0 : 3 * n],
            dst_ref=recv.at[0 : 3 * n],
            send_sem=send_sem.at[0],
            recv_sem=recv_sem.at[0],
            device_id=beside[1],
            device_id_type=MESH,
        )
        pl.when(sum(t.astype(jnp.int32) for t in there) == n)(every.wait_send)


def shards(
    displacement, velocity, modulus, gradient_map, trace_map, lift_map, split_map, spread_map,
    fracture_faces, fracture_counts,
):
    shape = displacement.shape
    flat = (shape[0] * 4, 128)
    args = (
        displacement.reshape(flat),
        velocity.reshape(flat),
        modulus.reshape(4, 128),
        gradient_map.T,
        trace_map,
        jnp.transpose(lift_map, (0, 2, 1)),
        split_map,
        jnp.transpose(spread_map, (0, 2, 1)),
        fracture_faces,
        fracture_counts,
    )
    vmem = pl.BlockSpec(memory_space=pltpu.VMEM)
    hbm = pl.BlockSpec(memory_space=pltpu.HBM)
    out = jax.ShapeDtypeStruct(flat, F32)
    opened, velocity_now, force = pl.pallas_call(
        kernel,
        out_shape=(out, out, out),
        in_specs=[hbm] * 10,
        out_specs=(vmem, vmem, vmem),
        scratch_shapes=[
            *(pltpu.VMEM(a.shape, a.dtype) for a in args),
            pltpu.VMEM((128, 512), F32),
            pltpu.VMEM((256, 512), BF16),
            pltpu.VMEM((928, 256), BF16),
            pltpu.VMEM((928, 128), BF16),
            pltpu.VMEM((64, 640), BF16),
            pltpu.VMEM((128, 640), BF16),
            pltpu.VMEM((128, 384), BF16),
            pltpu.VMEM((112, 128), BF16),
            pltpu.VMEM((112, 128), BF16),
            pltpu.VMEM((4, 64, 64), BF16),
            pltpu.VMEM((4, 64, 256), F32),
            pltpu.VMEM((4, 64, 256), BF16),
            pltpu.VMEM((6, 56, 128), F32),
            pltpu.VMEM((128, 256), F32),
            pltpu.VMEM((3, 128, 128), F32),
            pltpu.VMEM((3, 128, 128), F32),
            pltpu.VMEM((128, 128), F32),
            pltpu.VMEM((928, 512), F32),
            pltpu.VMEM((640, 512), BF16),
            pltpu.VMEM((640, 512), BF16),
            pltpu.VMEM((256, 512), BF16),
            pltpu.VMEM((256, 512), BF16),
            pltpu.VMEM((384, 512), BF16),
            pltpu.VMEM((384, 512), BF16),
            pltpu.VMEM((256, 512), BF16),
            pltpu.VMEM((128, 256), BF16),
            pltpu.VMEM((12, 56, 256), F32),
            pltpu.VMEM((12, 56, 256), F32),
            pltpu.SemaphoreType.DMA((1,)),
            pltpu.SemaphoreType.DMA((1,)),
            pltpu.SemaphoreType.DMA((7,)),
        ],
        compiler_params=pltpu.CompilerParams(
            collective_id=0, has_side_effects=True, vmem_limit_bytes=40 * 1024 * 1024
        ),
    )(*(pltpu.with_memory_space_constraint(a, pltpu.HBM) for a in args))
    velocity_out = velocity_now + substep * force
    displacement_out = opened + substep * velocity_out
    return displacement_out.reshape(shape), velocity_out.reshape(shape)


def solution(mesh):
    return jax.shard_map(
        shards,
        mesh=mesh,
        in_specs=(
            P(None, "px", "py", None),
            P(None, "px", "py", None),
            P("px", "py", None),
            P(),
            P(),
            P(),
            P(),
            P(),
            P(("px", "py"), None),
            P(("px", "py"), None),
        ),
        out_specs=(P(None, "px", "py", None), P(None, "px", "py", None)),
        check_vma=False,
    )
```

```python
import jax
import jax.numpy as jnp
from jax import lax
from jax.experimental import pallas as pl
from jax.experimental.pallas import tpu as pltpu
from jax.sharding import PartitionSpec as P

BLK_CAP = 128
penalty = 2.0
damping = 0.5
substep = 0.1
F32 = jnp.float32
BF16 = jnp.bfloat16
MESH = pl.DeviceIdType.MESH


def halves(value):
    high = value.astype(BF16)
    return high, (value - high.astype(F32)).astype(BF16)


def mm(a, b):
    return jnp.dot(a, b, preferred_element_type=F32)


def kernel(
    disp_in, vel_in, mod_in, grad_in, trace_in, lift_in, split_in, spread_in, faces_in, counts_in,
    out_u, out_w, out_f,
    disp, vel, mod, grad, trace, lift, split, spread, faces, counts,
    state, state_b, wa_h, wa_l, lb_h, lb_hl, ew_hl, cy, cx, cn, known, near, tp, gp, lp, pp, qp, proj,
    own_h, own_l, late_h, late_l, jump_h, jump_l, leap, e2,
    send, recv, in_sem, send_sem, recv_sem,
):
    px, py = lax.axis_index("px"), lax.axis_index("py")
    nx, ny = lax.axis_size("px"), lax.axis_size("py")
    odd = px % 2
    across, partner = px - 1 + 2 * odd, px + 1 - 2 * odd
    there = (
        jnp.logical_and(across >= 0, across < nx), partner >= 0, py > 0, py < ny - 1,
    )
    beside = ({"px": across}, {"px": partner}, {"py": py - 1}, {"py": py + 1})
    barrier = pltpu.get_barrier_semaphore()
    for side in (2, 3, 0, 1):

        @pl.when(there[side])
        def _(side=side):
            pl.semaphore_signal(barrier, inc=1, device_id=beside[side], device_id_type=MESH)

    def placed_face(f):
        return f + odd - 2 * f * odd if f < 2 else f

    def either(if_odd, if_even):
        return jnp.where(odd == 1, if_odd, if_even)

    names = ("trace", "disp", "vel", "grad", "lift", "mod", "spread", "split", "faces", "counts")
    given = (trace_in, disp_in, vel_in, grad_in, lift_in, mod_in, spread_in, split_in, faces_in, counts_in)
    local = (trace, disp, vel, grad, lift, mod, spread, split, faces, counts)
    loads = {}
    for n, name in enumerate(names):
        loads[name] = pltpu.make_async_copy(given[n], local[n], in_sem.at[0 if n < 3 else 1])
        loads[name].start()

    for ref in (state, tp, lp, pp, qp, gp):
        ref[...] = jnp.zeros_like(ref)
    for f in range(4):

        @pl.when(jnp.logical_not(there[f]))
        def _(f=f):
            for base in (0, 4, 8):
                recv[base + f] = jnp.zeros((56, 256), F32)

    def put_a(row, value):
        high, low = halves(value)
        rows = slice(row, row + value.shape[0])
        wa_h[rows, 0:128] = high
        wa_h[rows, 128:256] = high
        wa_l[rows, :] = low

    row_id = lax.broadcasted_iota(jnp.int32, (56, 128), 0)

    def face_rows(f, sign):
        both = tp[f]
        upper = penalty * both + (sign * 0.5) * pltpu.roll(both, 29, 0)
        upper = upper + pltpu.roll(damping * both, 64, 1)
        lower = jnp.where(row_id < 54, pltpu.roll(both, 27, 0), 0.0)
        return jnp.where(row_id < 27, upper, lower)

    def put_faces(row, d, sign):
        pair = [face_rows(2 * d, sign), face_rows(2 * d + 1, sign)]
        put_a(row + 112 * d, jnp.concatenate(pair, axis=0))

    for name in names[:3]:
        loads[name].wait()
    for f in range(6):
        tp[f, 0:54, 0:60] = trace[placed_face(f)]
    put_faces(0, 0, 1.0)
    put_faces(0, 1, 1.0)

    def block(k):
        return slice(128 * k, 128 * k + 128)

    for k in range(4):
        for row, ref in ((0, disp), (64, vel)):
            state[row : row + 60, block(k)] = either(
                ref[pl.ds(k ^ 2, 60, stride=4), :], ref[pl.ds(k, 60, stride=4), :]
            )

    def faced(f):
        return f if f < 2 else f ^ 1

    def copy(slot, columns=slice(0, 256)):
        return pltpu.make_async_remote_copy(
            src_ref=send.at[slot, :, columns],
            dst_ref=recv.at[slot - slot % 4 + faced(slot % 4), :, columns],
            send_sem=send_sem.at[0],
            recv_sem=recv_sem.at[min(slot // 4 * 3 + (0, 1, 2, 2)[slot % 4], 6)],
            device_id=beside[slot % 4],
            device_id_type=MESH,
        )

    def begin(*slots, columns=slice(0, 256)):
        for slot in slots:
            pl.when(there[slot % 4])(copy(slot, columns).start)

    def settle_x(s, f):
        pl.when(there[f])(copy(4 * s + f).wait_recv)

    def settle_y(s):
        both = there[2].astype(jnp.int32) + there[3].astype(jnp.int32)
        for n in (1, 2):
            every = pltpu.make_async_remote_copy(
                src_ref=send.at[0:n],
                dst_ref=recv.at[0:n],
                send_sem=send_sem.at[0],
                recv_sem=recv_sem.at[3 * s + 2],
                device_id=beside[1],
                device_id_type=MESH,
            )
            pl.when(both == n)(every.wait_recv)

    outer = ((0, 1), (2, 3), (0, 2), (1, 3))

    def split_state():
        for k in range(4):
            high, low = halves(state[:, block(k)])
            state_b[0:128, block(k)] = high
            state_b[128:256, block(k)] = low

    def project(rows):
        return mm(wa_h[rows, :], state_b[...]) + mm(wa_l[rows, :], state_b[0:128, :])

    split_state()
    for d in (1, 0):
        rows = slice(112 * d, 112 * d + 112)
        proj[rows, :] = project(rows)
        for f in (2 * d, 2 * d + 1):
            for half in range(2):
                send[f, :, block(half)] = proj[56 * f : 56 * f + 56, block(outer[f][half])]
        if d == 1:
            pl.semaphore_wait(barrier, sum(t.astype(jnp.int32) for t in there))
        begin(2 * d, 2 * d + 1)
    for ref in (late_h, late_l, leap):
        ref[...] = jnp.zeros_like(ref)
    put_faces(0, 2, 1.0)
    for d in range(3):
        put_faces(336, d, -1.0)
    for name in names[3:]:
        loads[name].wait()
    gp[0:60, 0:243] = grad[...]
    put_a(672, jnp.transpose(gp[...]))

    def put_b(column, value):
        high, low = halves(value)
        columns = slice(column, column + value.shape[1])
        lb_h[:, columns] = high
        lb_hl[0:64, columns] = high
        lb_hl[64:128, columns] = low

    put_b(384, -gp[0:64, :])
    lift_row = lax.broadcasted_iota(jnp.int32, (54, 60), 0)
    for f in range(6):
        at = 64 * (f % 2)
        lp[f // 2, at : at + 54, 0:60] = jnp.where(
            lift_row < 27, lift[placed_face(f)], 0.5 * lift[placed_face(f)]
        )
    for d in range(3):
        put_b(128 * d, jnp.transpose(lp[d])[0:64, :])

    reach = []
    for f in range(4):
        rows = face_rows(f, 1.0)
        reach.append((substep * substep) * rows + substep * pltpu.roll(rows, 64, 1))
    high, low = halves(jnp.concatenate(reach, axis=0)[:, 0:64])
    carry = mm(high, lb_h[:, 0:256]) + mm(low, lb_h[:, 0:256]) + mm(high, lb_hl[64:128, 0:256])
    cy[...] = carry[112:224, 0:128].astype(BF16)
    for f in range(2):
        pieces = [carry[56 * f : 56 * f + 56, 128:256], jnp.zeros((8, 128), F32)]
        cx[f] = jnp.concatenate(pieces, axis=0).astype(BF16)
    for f in range(4):
        o = f ^ 1
        pieces = [carry[56 * o : 56 * o + 56, 64 * o : 64 * o + 64], jnp.zeros((8, 64), F32)]
        cn[f] = jnp.concatenate(pieces, axis=0).astype(BF16)

    qp[0:27, 0:27] = split[...]
    qp[32:59, 0:27] = split[...]
    row128 = lax.broadcasted_iota(jnp.int32, (128, 128), 0)
    placed = jnp.where(row128 < 32, pltpu.roll(qp[...], 27, 1), pltpu.roll(qp[...], 91, 1))
    for f in range(6):
        at = 32 * (f % 2)
        pp[f // 2, at : at + 27, 0:60] = spread[placed_face(f)]
    lane64 = lax.broadcasted_iota(jnp.int32, (64, 128), 1)
    packed = jnp.zeros((64, 128), F32)
    for d in range(3):
        part = jnp.dot(
            jnp.transpose(pp[d])[0:64, :],
            placed,
            precision=lax.Precision.HIGHEST,
            preferred_element_type=F32,
        )
        high, low = halves(-part)
        ew_hl[0:64, block(d)] = high
        ew_hl[64:128, block(d)] = low
        if d < 2:
            first = jnp.where(lane64 < 64, -part, 0.0)
            packed += pltpu.roll(first, (104, 40)[d], 1)
            packed += pltpu.roll(-part - first, (72, 8)[d], 1)
    high, low = halves(packed)
    e2[0:64, 0:128] = high
    e2[0:64, 128:256] = high
    e2[64:128, 0:128] = low
    e2[64:128, 128:256] = jnp.zeros((64, 128), BF16)

    ids = faces[...]
    slots = lax.broadcasted_iota(jnp.int32, ids.shape, 1)
    section = jnp.where(slots < BLK_CAP, 0, jnp.where(slots < 2 * BLK_CAP, 1, 2))
    limit = jnp.where(
        section == 0,
        counts[0:1, 0:1],
        jnp.where(section == 1, BLK_CAP + counts[0:1, 1:2], 2 * BLK_CAP + counts[0:1, 2:3]),
    )
    group = ids >> 7
    group = jnp.where(group < 4, group, (group & 12) + ((group + 2 * odd) & 3))
    group = jnp.where(slots < limit, group, -1)
    spot = ids & 127
    high_hot = lax.broadcasted_iota(jnp.int32, (16, ids.shape[1]), 0) == group
    low_hot = lax.broadcasted_iota(jnp.int32, (128, ids.shape[1]), 0) == spot
    open_mask = lax.dot_general(
        high_hot.astype(F32).astype(BF16),
        low_hot.astype(F32).astype(BF16),
        (((1,), (1,)), ((), ())),
        preferred_element_type=F32,
    )

    alive = [jnp.where(t, 1.0, 0.0).astype(F32) for t in there]
    lane_row = lax.broadcasted_iota(jnp.int32, (1, 128), 1)
    not_first = (lane_row > 0).astype(F32)
    not_last = (lane_row < 127).astype(F32)

    gap = jnp.zeros((8, 128), F32)

    def put(high_ref, low_ref, row, k, value):
        high, low = halves(value)
        rows = slice(row, row + value.shape[0])
        high_ref[rows, block(k)] = high
        low_ref[rows, block(k)] = low

    def traced(f, k):
        return proj[56 * f : 56 * f + 56, block(k)]

    def own(f, k):
        return proj[336 + 56 * f : 392 + 56 * f, block(k)]

    def came(s, f, half):
        value = recv[4 * s + f, :, block(half)]
        if s > 0:
            value = value + known[f, 0:56, block(half)]
        return jnp.concatenate([value, gap], axis=0)

    def arrive(s, f):
        for half in range(2):
            value = came(s, f, half)
            late_h[64 * f : 64 * f + 64, block(outer[f][half])] = value.astype(BF16)

    def opens(f, k):
        i, j = k // 2, k % 2
        n = k if f > 3 else k ^ (2 - f // 2)
        inner = f > 3 or (i, 1 - i, j, 1 - j)[f] == 1
        if f == 4:
            return pltpu.roll(open_mask[8 + k : 9 + k, :], 1, 1)
        if f in (3, 5):
            row = 4 * (f // 2) + k
            return open_mask[row : row + 1, :]
        if f == 2:
            return open_mask[4 + n : 5 + n, :] if inner else recv[6, 54:55, block(i)]
        if inner:
            return open_mask[j : j + 1, :]
        mine, other = open_mask[2 + j : 3 + j, :], recv[4 + f, 54:55, block(j)]
        return either(mine, other) if f == 0 else either(other, mine)

    def mm3(both_ref, high_ref, columns, b_high, b_low):
        both = mm(both_ref[:, columns], b_high[...])
        return both[0:64] + both[64:128] + mm(high_ref[:, columns], b_low[...])

    early, lateral = slice(0, 640), slice(0, 256)
    moduli = [either(mod[k ^ 2 : (k ^ 2) + 1, :], mod[k : k + 1, :]) for k in range(4)]
    for s in range(3):
        if s > 0:
            for f in range(4):
                for half in range(2):
                    k = outer[f][half]
                    rest = came(s - 1, f, half) - late_h[64 * f : 64 * f + 64, block(k)].astype(F32)
                    late_l[64 * f : 64 * f + 64, block(k)] = rest.astype(BF16)
            force = mm3(lb_hl, lb_h, lateral, late_h, late_l)
            state[64:128, :] = state[64:128, :] + substep * force
            state[0:64, :] = state[0:64, :] + (substep * substep) * force
            split_state()
            for f in range(4):
                for half in range(2):
                    value = traced(f, outer[f][half]) * alive[f]
                    near[f, :, block(half)] = jnp.concatenate([value, gap], axis=0).astype(BF16)
                known[f] = mm(cn[f], near[f])
        todo = slice(224 if s == 0 else 0, 928)
        proj[todo, :] = project(todo)
        for k in range(4):
            i, j = k // 2, k % 2
            for d in range(3):
                n = k if d == 2 else k ^ (2 - d)
                part, jump = [], []
                for f in (2 * d, 2 * d + 1):
                    inner = d == 2 or (i, 1 - i, j, 1 - j)[f] == 1
                    if f == 4:
                        now = (pltpu.roll(traced(5, k), 1, 1) - own(4, k)) * not_first
                    elif f == 5:
                        now = (pltpu.roll(traced(4, k), 127, 1) - own(5, k)) * not_last
                    elif inner:
                        now = traced(f ^ 1, n) - own(f, k)
                    else:
                        now = own(f, k) * -alive[f]
                    part += [now, gap]
                    if s == 2:
                        jump += [now * opens(f, k), gap]
                put(own_h, own_l, 128 * d, k, jnp.concatenate(part, axis=0))
                if s == 2:
                    put(jump_h, jump_l, 128 * d, k, jnp.concatenate(jump, axis=0))
            put(own_h, own_l, 384, k, proj[672:928, block(k)] * moduli[k])
        force = mm3(lb_hl, lb_h, early, own_h, own_l)
        if s < 2:
            velocity = state[64:128, :] + substep * force
            state[64:128, :] = velocity
            state[0:64, :] = state[0:64, :] + substep * velocity
            split_state()
            ahead = project(slice(0, 224))
            for f in range(4):
                for half in range(2):
                    k = outer[f][half]
                    value = ahead[56 * f : 56 * f + 56, block(k)]
                    if s == 0 and f != 2:
                        row = 4 + k if f == 3 else 2 + half
                        value = jnp.where(row_id == 54, open_mask[row : row + 1, :], value)
                    send[4 * s + 4 + f, :, block(half)] = value
        else:
            moved = state[0:64, :] + mm3(ew_hl, ew_hl.at[0:64], slice(0, 384), jump_h, jump_l)
            for k in range(4):
                out_w[pl.ds(k, 60, stride=4), :] = either(
                    state[64:124, block(k ^ 2)], state[64:124, block(k)]
                )

        if s < 2:
            then = 4 * s + 4
            def after_x(f, s=s, then=then):
                settle_x(s, f)
                arrive(s, f)
                more = mm(cy[...], late_h[0:128, 256 * f : 256 * f + 256])
                for y in (2, 3):
                    at = 56 * (y - 2)
                    send[then + y, :, block(f)] = (
                        send[then + y, :, block(f)] + more[at : at + 56, block(y - 2)]
                    )
                begin(then + 2, then + 3, columns=block(f))

            def after_y(s=s, then=then):
                settle_y(s)
                for f in (2, 3):
                    arrive(s, f)
                for f in (0, 1):
                    more = mm(cx[f], late_h[128:256, 256 * f : 256 * f + 256])
                    send[then + f] = send[then + f] + more[0:56]
                    begin(then + f)

            @pl.when(odd == 0)
            def _():
                after_x(1)
                after_x(0)
                after_y()

            @pl.when(odd == 1)
            def _():
                after_y()
                after_x(1)
                after_x(0)

        else:
            every_side = sum(t.astype(jnp.int32) for t in there)
            for n in range(1, 5):
                every = pltpu.make_async_remote_copy(
                    src_ref=send.at[0:n],
                    dst_ref=recv.at[0:n],
                    send_sem=send_sem.at[0],
                    recv_sem=recv_sem.at[6],
                    device_id=beside[1],
                    device_id_type=MESH,
                )
                pl.when(every_side == n)(every.wait_recv)
            for f in range(4):
                for half in range(2):
                    k = outer[f][half]
                    value = came(2, f, half)
                    put(late_h, late_l, 64 * f, k, value)
                    high, low = halves(value[24:56] * opens(f, k))
                    leap[32 * f : 32 * f + 32, block(k)] = high
                    leap[128 + 32 * f : 160 + 32 * f, block(k)] = low
            force = force + mm3(lb_hl, lb_h, lateral, late_h, late_l)
            both = mm(e2[...], leap[...])
            moved = moved + both[0:64] + both[64:128]
            for k in range(4):
                out_u[pl.ds(k, 60, stride=4), :] = either(
                    moved[0:60, block(k ^ 2)], moved[0:60, block(k)]
                )
                out_f[pl.ds(k, 60, stride=4), :] = either(
                    force[0:60, block(k ^ 2)], force[0:60, block(k)]
                )

    for n in range(1, 5):
        every = pltpu.make_async_remote_copy(
            src_ref=send.at[0 : 3 * n],
            dst_ref=recv.at[0 : 3 * n],
            send_sem=send_sem.at[0],
            recv_sem=recv_sem.at[0],
            device_id=beside[1],
            device_id_type=MESH,
        )
        pl.when(sum(t.astype(jnp.int32) for t in there) == n)(every.wait_send)


def shards(
    displacement, velocity, modulus, gradient_map, trace_map, lift_map, split_map, spread_map,
    fracture_faces, fracture_counts,
):
    shape = displacement.shape
    flat = (shape[0] * 4, 128)
    args = (
        displacement.reshape(flat),
        velocity.reshape(flat),
        modulus.reshape(4, 128),
        gradient_map.T,
        trace_map,
        jnp.transpose(lift_map, (0, 2, 1)),
        split_map,
        jnp.transpose(spread_map, (0, 2, 1)),
        fracture_faces,
        fracture_counts,
    )
    vmem = pl.BlockSpec(memory_space=pltpu.VMEM)
    hbm = pl.BlockSpec(memory_space=pltpu.HBM)
    out = jax.ShapeDtypeStruct(flat, F32)
    opened, velocity_now, force = pl.pallas_call(
        kernel,
        out_shape=(out, out, out),
        in_specs=[hbm] * 10,
        out_specs=(vmem, vmem, vmem),
        scratch_shapes=[
            *(pltpu.VMEM(a.shape, a.dtype) for a in args),
            pltpu.VMEM((128, 512), F32),
            pltpu.VMEM((256, 512), BF16),
            pltpu.VMEM((928, 256), BF16),
            pltpu.VMEM((928, 128), BF16),
            pltpu.VMEM((64, 640), BF16),
            pltpu.VMEM((128, 640), BF16),
            pltpu.VMEM((128, 384), BF16),
            pltpu.VMEM((112, 128), BF16),
            pltpu.VMEM((2, 64, 128), BF16),
            pltpu.VMEM((4, 64, 64), BF16),
            pltpu.VMEM((4, 64, 256), F32),
            pltpu.VMEM((4, 64, 256), BF16),
            pltpu.VMEM((6, 56, 128), F32),
            pltpu.VMEM((128, 256), F32),
            pltpu.VMEM((3, 128, 128), F32),
            pltpu.VMEM((3, 128, 128), F32),
            pltpu.VMEM((128, 128), F32),
            pltpu.VMEM((928, 512), F32),
            pltpu.VMEM((640, 512), BF16),
            pltpu.VMEM((640, 512), BF16),
            pltpu.VMEM((256, 512), BF16),
            pltpu.VMEM((256, 512), BF16),
            pltpu.VMEM((384, 512), BF16),
            pltpu.VMEM((384, 512), BF16),
            pltpu.VMEM((256, 512), BF16),
            pltpu.VMEM((128, 256), BF16),
            pltpu.VMEM((12, 56, 256), F32),
            pltpu.VMEM((12, 56, 256), F32),
            pltpu.SemaphoreType.DMA((2,)),
            pltpu.SemaphoreType.DMA((1,)),
            pltpu.SemaphoreType.DMA((7,)),
        ],
        compiler_params=pltpu.CompilerParams(
            collective_id=0, has_side_effects=True, vmem_limit_bytes=40 * 1024 * 1024
        ),
    )(*(pltpu.with_memory_space_constraint(a, pltpu.HBM) for a in args))
    velocity_out = velocity_now + substep * force
    displacement_out = opened + substep * velocity_out
    return displacement_out.reshape(shape), velocity_out.reshape(shape)


def solution(mesh):
    return jax.shard_map(
        shards,
        mesh=mesh,
        in_specs=(
            P(None, "px", "py", None),
            P(None, "px", "py", None),
            P("px", "py", None),
            P(),
            P(),
            P(),
            P(),
            P(),
            P(("px", "py"), None),
            P(("px", "py"), None),
        ),
        out_specs=(P(None, "px", "py", None), P(None, "px", "py", None)),
        check_vma=False,
    )
```

```python
import jax
import jax.numpy as jnp
from jax import lax
from jax.experimental import pallas as pl
from jax.experimental.pallas import tpu as pltpu
from jax.sharding import PartitionSpec as P

BLK_CAP = 128
penalty = 2.0
damping = 0.5
substep = 0.1
F32 = jnp.float32
BF16 = jnp.bfloat16
MESH = pl.DeviceIdType.MESH


def halves(value):
    high = value.astype(BF16)
    return high, (value - high.astype(F32)).astype(BF16)


def mm(a, b):
    return jnp.dot(a, b, preferred_element_type=F32)


def kernel(
    disp_in, vel_in, mod_in, grad_in, trace_in, lift_in, split_in, spread_in, faces_in, counts_in,
    out_u, out_w, out_f,
    disp, vel, mod, grad, trace, lift, split, spread, faces, counts,
    state, state_b, wa_h, wa_l, lb_h, lb_hl, ew_hl, cy, cx, cn, known, near, tp, gp, lp, pp, qp, proj,
    own_h, own_l, late_h, late_l, jump_h, jump_l, leap, e2,
    send, recv, in_sem, send_sem, recv_sem,
):
    px, py = lax.axis_index("px"), lax.axis_index("py")
    nx, ny = lax.axis_size("px"), lax.axis_size("py")
    odd = px % 2
    across, partner = px - 1 + 2 * odd, px + 1 - 2 * odd
    there = (
        jnp.logical_and(across >= 0, across < nx), partner >= 0, py > 0, py < ny - 1,
    )
    beside = ({"px": across}, {"px": partner}, {"py": py - 1}, {"py": py + 1})
    barrier = pltpu.get_barrier_semaphore()
    for side in (2, 3, 0, 1):

        @pl.when(there[side])
        def _(side=side):
            pl.semaphore_signal(barrier, inc=1, device_id=beside[side], device_id_type=MESH)

    def placed_face(f):
        return f + odd - 2 * f * odd if f < 2 else f

    def either(if_odd, if_even):
        return jnp.where(odd == 1, if_odd, if_even)

    names = ("trace", "disp", "vel", "grad", "lift", "mod", "spread", "split", "faces", "counts")
    given = (trace_in, disp_in, vel_in, grad_in, lift_in, mod_in, spread_in, split_in, faces_in, counts_in)
    local = (trace, disp, vel, grad, lift, mod, spread, split, faces, counts)
    loads = {}
    for n, name in enumerate(names):
        loads[name] = pltpu.make_async_copy(given[n], local[n], in_sem.at[0 if n < 3 else 1])
        loads[name].start()

    for ref in (state, tp, lp, pp, qp, gp):
        ref[...] = jnp.zeros_like(ref)
    for f in range(4):

        @pl.when(jnp.logical_not(there[f]))
        def _(f=f):
            for base in (0, 4, 8):
                recv[base + f] = jnp.zeros((56, 256), F32)

    def put_a(row, value):
        high, low = halves(value)
        rows = slice(row, row + value.shape[0])
        wa_h[rows, 0:128] = high
        wa_h[rows, 128:256] = high
        wa_l[rows, :] = low

    row_id = lax.broadcasted_iota(jnp.int32, (56, 128), 0)

    def face_rows(f, sign):
        both = tp[f]
        upper = penalty * both + (sign * 0.5) * pltpu.roll(both, 29, 0)
        upper = upper + pltpu.roll(damping * both, 64, 1)
        lower = jnp.where(row_id < 54, pltpu.roll(both, 27, 0), 0.0)
        return jnp.where(row_id < 27, upper, lower)

    def put_faces(row, d, sign):
        pair = [face_rows(2 * d, sign), face_rows(2 * d + 1, sign)]
        put_a(row + 112 * d, jnp.concatenate(pair, axis=0))

    for name in names[:3]:
        loads[name].wait()
    for f in range(6):
        tp[f, 0:54, 0:60] = trace[placed_face(f)]
    put_faces(0, 0, 1.0)
    put_faces(0, 1, 1.0)

    def block(k):
        return slice(128 * k, 128 * k + 128)

    for k in range(4):
        for row, ref in ((0, disp), (64, vel)):
            state[row : row + 60, block(k)] = either(
                ref[pl.ds(k ^ 2, 60, stride=4), :], ref[pl.ds(k, 60, stride=4), :]
            )

    def faced(f):
        return f if f < 2 else f ^ 1

    def copy(slot, columns=slice(0, 256)):
        return pltpu.make_async_remote_copy(
            src_ref=send.at[slot, :, columns],
            dst_ref=recv.at[slot - slot % 4 + faced(slot % 4), :, columns],
            send_sem=send_sem.at[0],
            recv_sem=recv_sem.at[min(slot // 4 * 3 + (0, 1, 2, 2)[slot % 4], 6)],
            device_id=beside[slot % 4],
            device_id_type=MESH,
        )

    def begin(*slots, columns=slice(0, 256)):
        for slot in slots:
            pl.when(there[slot % 4])(copy(slot, columns).start)

    def settle_x(s, f):
        pl.when(there[f])(copy(4 * s + f).wait_recv)

    def settle_y(s):
        both = there[2].astype(jnp.int32) + there[3].astype(jnp.int32)
        for n in (1, 2):
            every = pltpu.make_async_remote_copy(
                src_ref=send.at[0:n],
                dst_ref=recv.at[0:n],
                send_sem=send_sem.at[0],
                recv_sem=recv_sem.at[3 * s + 2],
                device_id=beside[1],
                device_id_type=MESH,
            )
            pl.when(both == n)(every.wait_recv)

    outer = ((0, 1), (2, 3), (0, 2), (1, 3))

    def split_state():
        for k in range(4):
            high, low = halves(state[:, block(k)])
            state_b[0:128, block(k)] = high
            state_b[128:256, block(k)] = low

    def project(rows):
        return mm(wa_h[rows, :], state_b[...]) + mm(wa_l[rows, :], state_b[0:128, :])

    split_state()
    for d in (1, 0):
        rows = slice(112 * d, 112 * d + 112)
        proj[rows, :] = project(rows)
        for f in (2 * d, 2 * d + 1):
            for half in range(2):
                send[f, :, block(half)] = proj[56 * f : 56 * f + 56, block(outer[f][half])]
        if d == 1:
            pl.semaphore_wait(barrier, sum(t.astype(jnp.int32) for t in there))
        begin(2 * d, 2 * d + 1)
    for ref in (late_h, late_l, leap):
        ref[...] = jnp.zeros_like(ref)
    put_faces(0, 2, 1.0)
    for d in range(3):
        put_faces(336, d, -1.0)
    for name in names[3:]:
        loads[name].wait()
    gp[0:60, 0:243] = grad[...]
    put_a(672, jnp.transpose(gp[...]))

    def put_b(column, value):
        high, low = halves(value)
        columns = slice(column, column + value.shape[1])
        lb_h[:, columns] = high
        lb_hl[0:64, columns] = high
        lb_hl[64:128, columns] = low

    put_b(384, -gp[0:64, :])
    lift_row = lax.broadcasted_iota(jnp.int32, (54, 60), 0)
    for f in range(6):
        at = 64 * (f % 2)
        lp[f // 2, at : at + 54, 0:60] = jnp.where(
            lift_row < 27, lift[placed_face(f)], 0.5 * lift[placed_face(f)]
        )
    for d in range(3):
        put_b(128 * d, jnp.transpose(lp[d])[0:64, :])

    reach = []
    for f in range(4):
        rows = face_rows(f, 1.0)
        reach.append((substep * substep) * rows + substep * pltpu.roll(rows, 64, 1))
    high, low = halves(jnp.concatenate(reach, axis=0)[:, 0:64])
    carry = mm(high, lb_h[:, 0:256]) + mm(low, lb_h[:, 0:256]) + mm(high, lb_hl[64:128, 0:256])
    cy[...] = carry[112:224, 0:128].astype(BF16)
    cx[...] = carry[0:112, 128:256].astype(BF16)
    for f in range(4):
        o = f ^ 1
        pieces = [carry[56 * o : 56 * o + 56, 64 * o : 64 * o + 64], jnp.zeros((8, 64), F32)]
        cn[f] = jnp.concatenate(pieces, axis=0).astype(BF16)

    qp[0:27, 0:27] = split[...]
    qp[32:59, 0:27] = split[...]
    row128 = lax.broadcasted_iota(jnp.int32, (128, 128), 0)
    placed = jnp.where(row128 < 32, pltpu.roll(qp[...], 27, 1), pltpu.roll(qp[...], 91, 1))
    for f in range(6):
        at = 32 * (f % 2)
        pp[f // 2, at : at + 27, 0:60] = spread[placed_face(f)]
    lane64 = lax.broadcasted_iota(jnp.int32, (64, 128), 1)
    packed = jnp.zeros((64, 128), F32)
    for d in range(3):
        part = jnp.dot(
            jnp.transpose(pp[d])[0:64, :],
            placed,
            precision=lax.Precision.HIGHEST,
            preferred_element_type=F32,
        )
        high, low = halves(-part)
        ew_hl[0:64, block(d)] = high
        ew_hl[64:128, block(d)] = low
        if d < 2:
            first = jnp.where(lane64 < 64, -part, 0.0)
            packed += pltpu.roll(first, (104, 40)[d], 1)
            packed += pltpu.roll(-part - first, (72, 8)[d], 1)
    high, low = halves(packed)
    e2[0:64, 0:128] = high
    e2[0:64, 128:256] = high
    e2[64:128, 0:128] = low
    e2[64:128, 128:256] = jnp.zeros((64, 128), BF16)

    ids = faces[...]
    slots = lax.broadcasted_iota(jnp.int32, ids.shape, 1)
    section = jnp.where(slots < BLK_CAP, 0, jnp.where(slots < 2 * BLK_CAP, 1, 2))
    limit = jnp.where(
        section == 0,
        counts[0:1, 0:1],
        jnp.where(section == 1, BLK_CAP + counts[0:1, 1:2], 2 * BLK_CAP + counts[0:1, 2:3]),
    )
    group = ids >> 7
    group = jnp.where(group < 4, group, (group & 12) + ((group + 2 * odd) & 3))
    group = jnp.where(slots < limit, group, -1)
    spot = ids & 127
    high_hot = lax.broadcasted_iota(jnp.int32, (16, ids.shape[1]), 0) == group
    low_hot = lax.broadcasted_iota(jnp.int32, (128, ids.shape[1]), 0) == spot
    open_mask = lax.dot_general(
        high_hot.astype(F32).astype(BF16),
        low_hot.astype(F32).astype(BF16),
        (((1,), (1,)), ((), ())),
        preferred_element_type=F32,
    )

    alive = [jnp.where(t, 1.0, 0.0).astype(F32) for t in there]
    lane_row = lax.broadcasted_iota(jnp.int32, (1, 128), 1)
    not_first = (lane_row > 0).astype(F32)
    not_last = (lane_row < 127).astype(F32)

    gap = jnp.zeros((8, 128), F32)

    def put(high_ref, low_ref, row, k, value):
        high, low = halves(value)
        rows = slice(row, row + value.shape[0])
        high_ref[rows, block(k)] = high
        low_ref[rows, block(k)] = low

    def traced(f, k):
        return proj[56 * f : 56 * f + 56, block(k)]

    def own(f, k):
        return proj[336 + 56 * f : 392 + 56 * f, block(k)]

    def came(s, f, half):
        value = recv[4 * s + f, :, block(half)]
        if s > 0:
            value = value + known[f, 0:56, block(half)]
        return jnp.concatenate([value, gap], axis=0)

    def arrive(s, f):
        for half in range(2):
            value = came(s, f, half)
            late_h[64 * f : 64 * f + 64, block(outer[f][half])] = value.astype(BF16)

    def opens(f, k):
        i, j = k // 2, k % 2
        n = k if f > 3 else k ^ (2 - f // 2)
        inner = f > 3 or (i, 1 - i, j, 1 - j)[f] == 1
        if f == 4:
            return pltpu.roll(open_mask[8 + k : 9 + k, :], 1, 1)
        if f in (3, 5):
            row = 4 * (f // 2) + k
            return open_mask[row : row + 1, :]
        if f == 2:
            return open_mask[4 + n : 5 + n, :] if inner else recv[6, 54:55, block(i)]
        if inner:
            return open_mask[j : j + 1, :]
        mine, other = open_mask[2 + j : 3 + j, :], recv[4 + f, 54:55, block(j)]
        return either(mine, other) if f == 0 else either(other, mine)

    def mm3(both_ref, high_ref, columns, b_high, b_low):
        both = mm(both_ref[:, columns], b_high[...])
        return both[0:64] + both[64:128] + mm(high_ref[:, columns], b_low[...])

    early, lateral = slice(0, 640), slice(0, 256)
    moduli = [either(mod[k ^ 2 : (k ^ 2) + 1, :], mod[k : k + 1, :]) for k in range(4)]
    for s in range(3):
        if s > 0:
            for f in range(4):
                for half in range(2):
                    k = outer[f][half]
                    rest = came(s - 1, f, half) - late_h[64 * f : 64 * f + 64, block(k)].astype(F32)
                    late_l[64 * f : 64 * f + 64, block(k)] = rest.astype(BF16)
            force = mm3(lb_hl, lb_h, lateral, late_h, late_l)
            state[64:128, :] = state[64:128, :] + substep * force
            state[0:64, :] = state[0:64, :] + (substep * substep) * force
            split_state()
            for f in range(4):
                for half in range(2):
                    value = traced(f, outer[f][half]) * alive[f]
                    near[f, :, block(half)] = jnp.concatenate([value, gap], axis=0).astype(BF16)
                known[f] = mm(cn[f], near[f])
        todo = slice(224 if s == 0 else 0, 928)
        proj[todo, :] = project(todo)
        for k in range(4):
            i, j = k // 2, k % 2
            for d in range(3):
                n = k if d == 2 else k ^ (2 - d)
                part, jump = [], []
                for f in (2 * d, 2 * d + 1):
                    inner = d == 2 or (i, 1 - i, j, 1 - j)[f] == 1
                    if f == 4:
                        now = (pltpu.roll(traced(5, k), 1, 1) - own(4, k)) * not_first
                    elif f == 5:
                        now = (pltpu.roll(traced(4, k), 127, 1) - own(5, k)) * not_last
                    elif inner:
                        now = traced(f ^ 1, n) - own(f, k)
                    else:
                        now = own(f, k) * -alive[f]
                    part += [now, gap]
                    if s == 2:
                        jump += [now * opens(f, k), gap]
                put(own_h, own_l, 128 * d, k, jnp.concatenate(part, axis=0))
                if s == 2:
                    put(jump_h, jump_l, 128 * d, k, jnp.concatenate(jump, axis=0))
            put(own_h, own_l, 384, k, proj[672:928, block(k)] * moduli[k])
        force = mm3(lb_hl, lb_h, early, own_h, own_l)
        if s < 2:
            velocity = state[64:128, :] + substep * force
            state[64:128, :] = velocity
            state[0:64, :] = state[0:64, :] + substep * velocity
            split_state()
            ahead = project(slice(0, 224))
            for f in range(4):
                for half in range(2):
                    k = outer[f][half]
                    value = ahead[56 * f : 56 * f + 56, block(k)]
                    if s == 0 and f != 2:
                        row = 4 + k if f == 3 else 2 + half
                        value = jnp.where(row_id == 54, open_mask[row : row + 1, :], value)
                    send[4 * s + 4 + f, :, block(half)] = value
        else:
            moved = state[0:64, :] + mm3(ew_hl, ew_hl.at[0:64], slice(0, 384), jump_h, jump_l)
            for k in range(4):
                out_w[pl.ds(k, 60, stride=4), :] = either(
                    state[64:124, block(k ^ 2)], state[64:124, block(k)]
                )

        if s < 2:
            then = 4 * s + 4
            def after_x(f, s=s, then=then):
                settle_x(s, f)
                arrive(s, f)
                more = mm(cy[...], late_h[0:128, 256 * f : 256 * f + 256])
                for y in (2, 3):
                    at = 56 * (y - 2)
                    send[then + y, :, block(f)] = (
                        send[then + y, :, block(f)] + more[at : at + 56, block(y - 2)]
                    )
                begin(then + 2, then + 3, columns=block(f))

            def after_y(s=s, then=then):
                settle_y(s)
                for f in (2, 3):
                    arrive(s, f)
                more = mm(cx[...], late_h[128:256, :])
                for f in (0, 1):
                    at = 56 * f
                    send[then + f] = send[then + f] + more[at : at + 56, 256 * f : 256 * f + 256]
                begin(then, then + 1)

            after_x(1)

            @pl.when(odd == 0)
            def _():
                after_x(0)
                after_y()

            @pl.when(odd == 1)
            def _():
                after_y()
                after_x(0)

        else:
            every_side = sum(t.astype(jnp.int32) for t in there)
            for n in range(1, 5):
                every = pltpu.make_async_remote_copy(
                    src_ref=send.at[0:n],
                    dst_ref=recv.at[0:n],
                    send_sem=send_sem.at[0],
                    recv_sem=recv_sem.at[6],
                    device_id=beside[1],
                    device_id_type=MESH,
                )
                pl.when(every_side == n)(every.wait_recv)
            for f in range(4):
                for half in range(2):
                    k = outer[f][half]
                    value = came(2, f, half)
                    put(late_h, late_l, 64 * f, k, value)
                    high, low = halves(value[24:56] * opens(f, k))
                    leap[32 * f : 32 * f + 32, block(k)] = high
                    leap[128 + 32 * f : 160 + 32 * f, block(k)] = low
            force = force + mm3(lb_hl, lb_h, lateral, late_h, late_l)
            both = mm(e2[...], leap[...])
            moved = moved + both[0:64] + both[64:128]
            for k in range(4):
                out_u[pl.ds(k, 60, stride=4), :] = either(
                    moved[0:60, block(k ^ 2)], moved[0:60, block(k)]
                )
                out_f[pl.ds(k, 60, stride=4), :] = either(
                    force[0:60, block(k ^ 2)], force[0:60, block(k)]
                )

    for n in range(1, 5):
        every = pltpu.make_async_remote_copy(
            src_ref=send.at[0 : 3 * n],
            dst_ref=recv.at[0 : 3 * n],
            send_sem=send_sem.at[0],
            recv_sem=recv_sem.at[0],
            device_id=beside[1],
            device_id_type=MESH,
        )
        pl.when(sum(t.astype(jnp.int32) for t in there) == n)(every.wait_send)


def shards(
    displacement, velocity, modulus, gradient_map, trace_map, lift_map, split_map, spread_map,
    fracture_faces, fracture_counts,
):
    shape = displacement.shape
    flat = (shape[0] * 4, 128)
    args = (
        displacement.reshape(flat),
        velocity.reshape(flat),
        modulus.reshape(4, 128),
        gradient_map.T,
        trace_map,
        jnp.transpose(lift_map, (0, 2, 1)),
        split_map,
        jnp.transpose(spread_map, (0, 2, 1)),
        fracture_faces,
        fracture_counts,
    )
    vmem = pl.BlockSpec(memory_space=pltpu.VMEM)
    hbm = pl.BlockSpec(memory_space=pltpu.HBM)
    out = jax.ShapeDtypeStruct(flat, F32)
    opened, velocity_now, force = pl.pallas_call(
        kernel,
        out_shape=(out, out, out),
        in_specs=[hbm] * 10,
        out_specs=(vmem, vmem, vmem),
        scratch_shapes=[
            *(pltpu.VMEM(a.shape, a.dtype) for a in args),
            pltpu.VMEM((128, 512), F32),
            pltpu.VMEM((256, 512), BF16),
            pltpu.VMEM((928, 256), BF16),
            pltpu.VMEM((928, 128), BF16),
            pltpu.VMEM((64, 640), BF16),
            pltpu.VMEM((128, 640), BF16),
            pltpu.VMEM((128, 384), BF16),
            pltpu.VMEM((112, 128), BF16),
            pltpu.VMEM((112, 128), BF16),
            pltpu.VMEM((4, 64, 64), BF16),
            pltpu.VMEM((4, 64, 256), F32),
            pltpu.VMEM((4, 64, 256), BF16),
            pltpu.VMEM((6, 56, 128), F32),
            pltpu.VMEM((128, 256), F32),
            pltpu.VMEM((3, 128, 128), F32),
            pltpu.VMEM((3, 128, 128), F32),
            pltpu.VMEM((128, 128), F32),
            pltpu.VMEM((928, 512), F32),
            pltpu.VMEM((640, 512), BF16),
            pltpu.VMEM((640, 512), BF16),
            pltpu.VMEM((256, 512), BF16),
            pltpu.VMEM((256, 512), BF16),
            pltpu.VMEM((384, 512), BF16),
            pltpu.VMEM((384, 512), BF16),
            pltpu.VMEM((256, 512), BF16),
            pltpu.VMEM((128, 256), BF16),
            pltpu.VMEM((12, 56, 256), F32),
            pltpu.VMEM((12, 56, 256), F32),
            pltpu.SemaphoreType.DMA((2,)),
            pltpu.SemaphoreType.DMA((1,)),
            pltpu.SemaphoreType.DMA((7,)),
        ],
        compiler_params=pltpu.CompilerParams(
            collective_id=0, has_side_effects=True, vmem_limit_bytes=40 * 1024 * 1024
        ),
    )(*(pltpu.with_memory_space_constraint(a, pltpu.HBM) for a in args))
    velocity_out = velocity_now + substep * force
    displacement_out = opened + substep * velocity_out
    return displacement_out.reshape(shape), velocity_out.reshape(shape)


def solution(mesh):
    return jax.shard_map(
        shards,
        mesh=mesh,
        in_specs=(
            P(None, "px", "py", None),
            P(None, "px", "py", None),
            P("px", "py", None),
            P(),
            P(),
            P(),
            P(),
            P(),
            P(("px", "py"), None),
            P(("px", "py"), None),
        ),
        out_specs=(P(None, "px", "py", None), P(None, "px", "py", None)),
        check_vma=False,
    )
```
